256 devices in a mesh: tok: 32 (over x, z_hi, core), hid: 8 (over y, z_lo).
Axes of the slice: x: 4, y: 4, z: 8 (z_hi: 4, z_lo: 2; z = z_hi * 2 + z_lo), core: 2. Of those that a mesh axis runs over, the one named last changes fastest.
Arguments:
- base: float32 [1024, 16384], P('tok', 'hid'), may hold values from -6 to 6
- source: float32 [1024, 16384], P('tok', 'hid'), may hold values from -6 to 6
- pairs: int32 [1024], replicated, may hold values from 0 to 1023, each once
- counts: int32 [1024], replicated, may hold values from 1 to 128
- rotation: float32 [16384, 16384], P('hid', 'tok'), may hold values from -0.046875 to 0.046875
Outputs:
- patched: float32 [1024, 16384], P('tok', 'hid')
The draws below stay inside these ranges and needn't reach their ends.
All inputs are finite; a program needn't handle non-finite values.
Results may differ from the reference program's by a relative error of at most 0.000075.
Values sent between devices are 32-bit elements; how exact they have to be, the bound alone decides.
No kernel may reach another device: no remote copies, remote signals or barrier semaphores. Data moves between devices by JAX's collectives and lax.ppermute only.
A program may use at most 64 MiB of HBM per device.

```python
import jax
import jax.numpy as jnp
from jax import lax

D = 16384
BLOCK = 128
ROWS = 1024


def set_ends(drawn, rng, smallest, high):
    longest = drawn.shape.index(max(drawn.shape))
    spots = []
    for shift in (0, 1):
        where = [jax.random.randint(jax.random.fold_in(rng, axis), (), 0, length) for axis, length in enumerate(drawn.shape)]
        where[longest] = (where[longest] + shift) % drawn.shape[longest]
        spots.append(tuple(where))
    return drawn.at[spots[0]].set(smallest).at[spots[1]].set(high)


def shard_levels(rng, dims, cuts, smallest, top_value):
    level = 1.0
    for position, blocks in cuts:
        steps = jax.random.uniform(jax.random.fold_in(jax.random.fold_in(rng, 6), position), (blocks,), jnp.float32, smallest / len(cuts), top_value / len(cuts))
        level = level * jnp.repeat(jnp.exp(steps), dims[position] // blocks).reshape((-1,) + (1,) * (len(dims) - 1 - position))
    return level


def scatter_about(key, shape, deviation, limit, shards=(), held_as=jnp.bfloat16):
    factor_of = shard_levels(key, shape, shards, -0.22, 0.18) if shards else 1.0
    drawn = jax.random.normal(key, shape, jnp.float32) * deviation * factor_of
    return jnp.minimum(jnp.maximum(drawn, -limit), limit).astype(held_as)


def setup_inputs(seed: int = 0) -> dict:
    key_of = jax.random.split(jax.random.key(seed), 6)
    return {
        "base": scatter_about(key_of[0], (ROWS, D), 1.0, 6.0, ((0, 32), (1, 8)), jnp.float32),
        "source": scatter_about(key_of[1], (ROWS, D), 1.0, 6.0, ((0, 32), (1, 8)), jnp.float32),
        "pairs": jax.random.permutation(key_of[2], ROWS).astype(jnp.int32),
        "counts": set_ends(jax.random.randint(key_of[3], (ROWS,), 1, D // BLOCK + 1), jax.random.fold_in(key_of[3], 1), 1, (D // BLOCK + 1) - 1).astype(jnp.int32),
        "rotation": scatter_about(key_of[4], (D, D), D ** -0.5, 0.046875, ((0, 8), (1, 32)), jnp.float32),
    }


def reference(base, source, pairs, counts, rotation):
    highest = lax.Precision.HIGHEST
    rotated_base = jnp.dot(base, rotation, precision=highest, preferred_element_type=jnp.float32)
    paired = jnp.take(source, pairs.astype(jnp.int32), axis=0)
    rotated_source = jnp.dot(paired, rotation, precision=highest, preferred_element_type=jnp.float32)
    columns = jnp.arange(D, dtype=jnp.int32)
    limits = counts.astype(jnp.int32) * BLOCK
    mixed = jnp.where(columns[None, :] < limits[:, None], rotated_source, rotated_base)
    return lax.dot_general(mixed, rotation, (((1,), (1,)), ((), ())), precision=highest, preferred_element_type=jnp.float32)
```

```python
import jax
import jax.numpy as jnp
from jax import lax
from jax.sharding import PartitionSpec as P

BLOCK = 128


def local(base, source, pairs, counts, rotation):
    high = lax.Precision.HIGH
    stacked = jnp.stack([base, source])
    terms = jnp.einsum(
        "srk,kc->src",
        lax.all_gather(stacked, "tok", axis=1, tiled=True),
        rotation,
        precision=high,
        preferred_element_type=jnp.float32,
    )
    width = rotation.shape[1]
    columns = lax.axis_index("tok") * width + jnp.arange(width, dtype=jnp.int32)
    source_terms = terms[1].at[pairs].get(mode="promise_in_bounds")
    chosen = columns[None, :] < (counts * BLOCK)[:, None]
    mixed_terms = jnp.where(chosen, source_terms, terms[0])
    mixed = lax.psum_scatter(mixed_terms, "hid", scatter_dimension=0, tiled=True)
    full = lax.all_gather(mixed, "hid", axis=0, tiled=True)
    return lax.psum_scatter(
        lax.dot_general(
            full,
            rotation,
            (((1,), (1,)), ((), ())),
            precision=high,
            preferred_element_type=jnp.float32,
        ),
        "tok",
        scatter_dimension=0,
        tiled=True,
    )


def solution(mesh):
    return jax.shard_map(
        local,
        mesh=mesh,
        in_specs=(P("tok", "hid"), P("tok", "hid"), P(), P(), P("hid", "tok")),
        out_specs=P("tok", "hid"),
        check_vma=False,
    )
```

```python
import jax
import jax.numpy as jnp
from jax import lax
from jax.sharding import Mesh, PartitionSpec as P

BLOCK = 128
SIZES = {"x": 4, "zh": 4, "c": 2, "y": 4, "zl": 2}
CHUNKS = 2


def fetch(a, axis, d):
    n = SIZES[axis]
    return lax.ppermute(a, axis, [((i + d) % n, i) for i in range(n)])


def ring_gather(own, axis):
    half = own.shape[0] // 2
    ahead = fetch(own, axis, 1)
    behind = fetch(own, axis, -1)
    far = [fetch(ahead[:half], axis, 1), fetch(behind[half:], axis, -1)]
    return jnp.concatenate([own, ahead, *far, behind], axis=0)


def ring_scatter(terms, axis):
    rows = terms.shape[0] // 4
    half = rows // 2
    own, ahead, far, behind = (terms[i * rows : (i + 1) * rows] for i in range(4))
    to_ahead = fetch(far[:half], axis, -1)
    to_behind = fetch(far[half:], axis, 1)
    ahead = jnp.concatenate([ahead[:half] + to_ahead, ahead[half:]], axis=0)
    behind = jnp.concatenate([behind[:half], behind[half:] + to_behind], axis=0)
    return own + fetch(ahead, axis, -1) + fetch(behind, axis, 1)


def dot(a, b, dims):
    return lax.dot_general(
        a, b, (dims, ((), ())), precision=lax.Precision.HIGH, preferred_element_type=jnp.float32
    )


def part(a, index, size):
    return lax.dynamic_slice_in_dim(a, index * size, size, 0)


def local(base, source, pairs, counts, rotation):
    x, zh, c, y, zl = (lax.axis_index(a) for a in ("x", "zh", "c", "y", "zl"))
    features = rotation.shape[0] // 2
    width = rotation.shape[1]
    rows = base.shape[0]

    with jax.named_scope("core_swap_in"):
        both = jnp.concatenate([base, source], axis=0)
        halves = both.reshape(2 * rows, 2, features)
        mine = lax.dynamic_index_in_dim(halves, c, 1, keepdims=False)
        theirs = fetch(lax.dynamic_index_in_dim(halves, 1 - c, 1, keepdims=False), "c", 1)
        first = jnp.where(c == 0, mine, theirs)
        second = jnp.where(c == 0, theirs, mine)
        base_parts = [first[:rows], second[:rows]]
        source_parts = [first[rows:], second[rows:]]
        matrix = jnp.concatenate(
            [part(rotation, c, features), fetch(part(rotation, 1 - c, features), "c", 1)], axis=1
        )

    def gather(own):
        return ring_gather(ring_gather(own, "zh"), "x")

    steps = jnp.arange(4, dtype=jnp.int32)
    at_x = (x + steps) % 4
    at_z = (zh + steps) % 4
    tok = (x * 4 + zh) * 2
    lane = jnp.arange(width, dtype=jnp.int32)
    columns = jnp.concatenate([(tok + c) * width + lane, (tok + 1 - c) * width + lane])

    with jax.named_scope("source_terms"):
        source_terms = jnp.concatenate(
            [dot(gather(own), matrix, ((1,), (0,))) for own in source_parts], axis=0
        )

    out = []
    for k in range(CHUNKS):
        with jax.named_scope(f"base_terms_{k}"):
            base_terms = dot(gather(base_parts[k]), matrix, ((1,), (0,)))
        with jax.named_scope(f"select_{k}"):
            ids = (
                at_x[:, None, None] * 256
                + at_z[None, :, None] * 64
                + k * rows
                + jnp.arange(rows, dtype=jnp.int32)[None, None, :]
            ).reshape(-1)
            wanted = pairs[ids]
            spot = (
                (wanted // rows) % 2 * (16 * rows)
                + (wanted // 256 - x) % 4 * (4 * rows)
                + (wanted // 64 - zh) % 4 * rows
                + wanted % rows
            )
            limits = counts[ids] * BLOCK
            taken = source_terms.at[spot].get(mode="promise_in_bounds")
            mixed = jnp.where(columns[None, :] < limits[:, None], taken, base_terms)
        with jax.named_scope(f"reduce_hid_{k}"):
            mixed = mixed[:, :width] + fetch(mixed[:, width:], "c", 1)
            share = mixed.shape[0] // 4
            mixed = part(mixed, y, share) + sum(
                fetch(part(mixed, (y - d) % 4, share), "y", d) for d in (1, 2, 3)
            )
            share = share // 2
            mixed = part(mixed, zl, share) + fetch(part(mixed, 1 - zl, share), "zl", 1)
        with jax.named_scope(f"gather_hid_{k}"):
            other = fetch(mixed, "zl", 1)
            mixed = jnp.where(
                zl == 0,
                jnp.concatenate([mixed, other], axis=0),
                jnp.concatenate([other, mixed], axis=0),
            )
            full = jnp.zeros((4 * mixed.shape[0], width), jnp.float32)
            for d in range(4):
                block = mixed if d == 0 else fetch(mixed, "y", d)
                full = lax.dynamic_update_slice_in_dim(
                    full, block, (y + d) % 4 * mixed.shape[0], 0
                )
            full = jnp.concatenate([full, fetch(full, "c", 1)], axis=1)
        with jax.named_scope(f"inverse_{k}"):
            terms = dot(full, matrix, ((1,), (1,)))
            out.append(ring_scatter(ring_scatter(terms, "x"), "zh"))

    with jax.named_scope("core_swap_out"):
        mine = jnp.where(c == 0, out[0], out[1])
        theirs = fetch(jnp.where(c == 0, out[1], out[0]), "c", 1)
        return jnp.where(
            c == 0,
            jnp.concatenate([mine, theirs], axis=1),
            jnp.concatenate([theirs, mine], axis=1),
        )


def solution(mesh):
    fine = Mesh(mesh.devices.reshape(4, 4, 2, 4, 2), ("x", "zh", "c", "y", "zl"))
    tok, hid = ("x", "zh", "c"), ("y", "zl")
    return jax.shard_map(
        local,
        mesh=fine,
        in_specs=(P(tok, hid), P(tok, hid), P(), P(), P(hid, tok)),
        out_specs=P(tok, hid),
        check_vma=False,
    )
```

```python
import jax
import jax.numpy as jnp
from jax import lax
from jax.sharding import Mesh, PartitionSpec as P

BLOCK = 128
SIZES = {"x": 4, "zh": 4, "c": 2, "y": 4, "zl": 2}
CHUNKS = 2


def fetch(a, axis, d):
    n = SIZES[axis]
    return lax.ppermute(a, axis, [((i + d) % n, i) for i in range(n)])


def direct_gather(own, axis):
    return jnp.concatenate([own, *(fetch(own, axis, d) for d in (1, 2, 3))], axis=0)


def neighbours(own, axis):
    return own, fetch(own, axis, 1), fetch(own, axis, -1)


def finish_ring(own, ahead, behind, axis):
    half = own.shape[0] // 2
    far = [fetch(ahead[:half], axis, 1), fetch(behind[half:], axis, -1)]
    return jnp.concatenate([own, ahead, *far, behind], axis=0)


def after(a, *others):
    return lax.optimization_barrier((a, *others))


def ring_scatter(terms, axis):
    rows = terms.shape[0] // 4
    half = rows // 2
    own, ahead, far, behind = (terms[i * rows : (i + 1) * rows] for i in range(4))
    to_ahead = fetch(far[:half], axis, -1)
    to_behind = fetch(far[half:], axis, 1)
    ahead = jnp.concatenate([ahead[:half] + to_ahead, ahead[half:]], axis=0)
    behind = jnp.concatenate([behind[:half], behind[half:] + to_behind], axis=0)
    return own + fetch(ahead, axis, -1) + fetch(behind, axis, 1)


def dot(a, b, dims):
    return lax.dot_general(
        a, b, (dims, ((), ())), precision=lax.Precision.HIGH, preferred_element_type=jnp.float32
    )


def part(a, index, size):
    return lax.dynamic_slice_in_dim(a, index * size, size, 0)


def local(base, source, pairs, counts, rotation):
    x, zh, c, y, zl = (lax.axis_index(a) for a in ("x", "zh", "c", "y", "zl"))
    features = rotation.shape[0] // 2
    width = rotation.shape[1]
    rows = base.shape[0]

    with jax.named_scope("core_swap_in"):
        both = jnp.concatenate([base, source], axis=0)
        halves = both.reshape(2 * rows, 2, features)
        mine = lax.dynamic_index_in_dim(halves, c, 1, keepdims=False)
        theirs = fetch(lax.dynamic_index_in_dim(halves, 1 - c, 1, keepdims=False), "c", 1)
        first = jnp.where(c == 0, mine, theirs)
        second = jnp.where(c == 0, theirs, mine)
        base_parts = [first[:rows], second[:rows]]
        source_parts = [first[rows:], second[rows:]]
        matrix = jnp.concatenate(
            [part(rotation, c, features), fetch(part(rotation, 1 - c, features), "c", 1)], axis=1
        )

    steps = jnp.arange(4, dtype=jnp.int32)
    at_x = (x + steps) % 4
    at_z = (zh + steps) % 4
    tok = (x * 4 + zh) * 2
    lane = jnp.arange(width, dtype=jnp.int32)
    columns = jnp.concatenate([(tok + c) * width + lane, (tok + 1 - c) * width + lane])

    with jax.named_scope("gather_tok"):
        near = []
        last = None
        for own in [*source_parts, *base_parts]:
            if last is not None:
                own, last = after(own, last)
                near[-1] = last
            last = direct_gather(own, "zh")
            near.append(last)
        gathered = []
        last = None
        for own in near:
            if last is not None:
                own, *last = after(own, *last)
                gathered.append(finish_ring(*last, "x"))
            last = neighbours(own, "x")
        gathered.append(finish_ring(*last, "x"))

    with jax.named_scope("source_terms"):
        source_terms = jnp.concatenate(
            [dot(g, matrix, ((1,), (0,))) for g in gathered[:2]], axis=0
        )

    out = []
    for k in range(CHUNKS):
        with jax.named_scope(f"base_terms_{k}"):
            base_terms = dot(gathered[2 + k], matrix, ((1,), (0,)))
        with jax.named_scope(f"select_{k}"):
            ids = (
                at_x[:, None, None] * 256
                + at_z[None, :, None] * 64
                + k * rows
                + jnp.arange(rows, dtype=jnp.int32)[None, None, :]
            ).reshape(-1)
            wanted = pairs[ids]
            spot = (
                (wanted // rows) % 2 * (16 * rows)
                + (wanted // 256 - x) % 4 * (4 * rows)
                + (wanted // 64 - zh) % 4 * rows
                + wanted % rows
            )
            limits = counts[ids] * BLOCK
            taken = source_terms.at[spot].get(mode="promise_in_bounds")
            mixed = jnp.where(columns[None, :] < limits[:, None], taken, base_terms)
        with jax.named_scope(f"reduce_hid_{k}"):
            mixed = mixed[:, :width] + fetch(mixed[:, width:], "c", 1)
            if k + 1 < CHUNKS:
                mixed, gathered[3 + k] = after(mixed, gathered[3 + k])
            share = mixed.shape[0] // 4
            mixed = part(mixed, y, share) + sum(
                fetch(part(mixed, (y - d) % 4, share), "y", d) for d in (1, 2, 3)
            )
            share = share // 2
            mixed = part(mixed, zl, share) + fetch(part(mixed, 1 - zl, share), "zl", 1)
        with jax.named_scope(f"gather_hid_{k}"):
            other = fetch(mixed, "zl", 1)
            mixed = jnp.where(
                zl == 0,
                jnp.concatenate([mixed, other], axis=0),
                jnp.concatenate([other, mixed], axis=0),
            )
            full = jnp.zeros((4 * mixed.shape[0], width), jnp.float32)
            for d in range(4):
                block = mixed if d == 0 else fetch(mixed, "y", d)
                full = lax.dynamic_update_slice_in_dim(
                    full, block, (y + d) % 4 * mixed.shape[0], 0
                )
            full = jnp.concatenate([full, fetch(full, "c", 1)], axis=1)
        with jax.named_scope(f"inverse_{k}"):
            terms = dot(full, matrix, ((1,), (1,)))
            out.append(ring_scatter(ring_scatter(terms, "x"), "zh"))

    with jax.named_scope("core_swap_out"):
        mine = jnp.where(c == 0, out[0], out[1])
        theirs = fetch(jnp.where(c == 0, out[1], out[0]), "c", 1)
        return jnp.where(
            c == 0,
            jnp.concatenate([mine, theirs], axis=1),
            jnp.concatenate([theirs, mine], axis=1),
        )


def solution(mesh):
    fine = Mesh(mesh.devices.reshape(4, 4, 2, 4, 2), ("x", "zh", "c", "y", "zl"))
    tok, hid = ("x", "zh", "c"), ("y", "zl")
    return jax.shard_map(
        local,
        mesh=fine,
        in_specs=(P(tok, hid), P(tok, hid), P(), P(), P(hid, tok)),
        out_specs=P(tok, hid),
        check_vma=False,
    )
```

```python
import jax
import jax.numpy as jnp
from jax import lax
from jax.sharding import Mesh, PartitionSpec as P

BLOCK = 128
SIZES = {"x": 4, "zh": 4, "c": 2, "y": 4, "zl": 2}
HID = ("y", "zl")


def fetch(a, axis, d):
    n = SIZES[axis]
    return lax.ppermute(a, axis, [((i + d) % n, i) for i in range(n)])


def ring_gather(own, axis):
    half = own.shape[0] // 2
    ahead = fetch(own, axis, 1)
    behind = fetch(own, axis, -1)
    far = [fetch(ahead[:half], axis, 1), fetch(behind[half:], axis, -1)]
    return jnp.concatenate([own, ahead, *far, behind], axis=0)


def part(a, index, size):
    return lax.dynamic_slice_in_dim(a, index * size, size, 0)


def ring_scatter(terms, axis):
    me = lax.axis_index(axis)
    rows = terms.shape[0] // 4
    half = rows // 2
    own, ahead, far, behind = (part(terms, (me + d) % 4, rows) for d in range(4))
    to_ahead = fetch(far[:half], axis, -1)
    to_behind = fetch(far[half:], axis, 1)
    ahead = jnp.concatenate([ahead[:half] + to_ahead, ahead[half:]], axis=0)
    behind = jnp.concatenate([behind[:half], behind[half:] + to_behind], axis=0)
    return own + fetch(ahead, axis, -1) + fetch(behind, axis, 1)


def dot(a, b, dims):
    return lax.dot_general(
        a, b, (dims, ((), ())), precision=lax.Precision.HIGH, preferred_element_type=jnp.float32
    )


def local(base, source, pairs, counts, rotation):
    x, zh, c = (lax.axis_index(a) for a in ("x", "zh", "c"))
    features = rotation.shape[0] // 2
    width = rotation.shape[1]
    rows = base.shape[0]

    with jax.named_scope("core_swap_in"):
        both = jnp.concatenate([base, source], axis=0)
        mine = lax.dynamic_slice_in_dim(both, c * features, features, 1)
        theirs = fetch(lax.dynamic_slice_in_dim(both, (1 - c) * features, features, 1), "c", 1)
        first = jnp.where(c == 0, mine, theirs)
        second = jnp.where(c == 0, theirs, mine)
        matrix = jnp.concatenate(
            [part(rotation, c, features), fetch(part(rotation, 1 - c, features), "c", 1)], axis=1
        )

    with jax.named_scope("gather_base"):
        chip_base = jnp.concatenate([first[:rows], second[:rows]], axis=0)
        base_all = lax.all_gather(chip_base, ("x", "zh"), axis=0, tiled=True)

    with jax.named_scope("source_terms"):
        source_terms = jnp.concatenate(
            [
                dot(ring_gather(ring_gather(own, "zh"), "x"), matrix, ((1,), (0,)))
                for own in (first[rows:], second[rows:])
            ],
            axis=0,
        )

    with jax.named_scope("base_terms"):
        base_terms = dot(base_all, matrix, ((1,), (0,)))

    with jax.named_scope("select"):
        tok = (x * 4 + zh) * 2
        lane = jnp.arange(width, dtype=jnp.int32)
        columns = jnp.concatenate([(tok + c) * width + lane, (tok + 1 - c) * width + lane])
        spot = (
            (pairs // rows) % 2 * (16 * rows)
            + (pairs // 256 - x) % 4 * (4 * rows)
            + (pairs // 64 - zh) % 4 * rows
            + pairs % rows
        )
        taken = source_terms.at[spot].get(mode="promise_in_bounds")
        mixed = jnp.where(columns[None, :] < (counts * BLOCK)[:, None], taken, base_terms)

    with jax.named_scope("reduce_hid"):
        mixed = mixed[:, :width] + fetch(mixed[:, width:], "c", 1)
        share = mixed.shape[0] // 8
        mixed = lax.all_to_all(mixed.reshape(8, share, width), HID, 0, 0)
        mixed = mixed.sum(axis=0)
    with jax.named_scope("gather_hid"):
        full = lax.all_to_all(jnp.broadcast_to(mixed, (8, share, width)), HID, 0, 0)
        full = full.reshape(8 * share, width)
        other = fetch(full, "c", 1)

    with jax.named_scope("inverse"):
        terms = dot(jnp.concatenate([full, other], axis=1), matrix, ((1,), (1,)))
    with jax.named_scope("scatter"):
        out = ring_scatter(ring_scatter(terms, "x"), "zh")

    with jax.named_scope("core_swap_out"):
        mine = part(out, c, rows)
        theirs = fetch(part(out, 1 - c, rows), "c", 1)
        return jnp.where(
            c == 0,
            jnp.concatenate([mine, theirs], axis=1),
            jnp.concatenate([theirs, mine], axis=1),
        )


def solution(mesh):
    fine = Mesh(mesh.devices.reshape(4, 4, 2, 4, 2), ("x", "zh", "c", "y", "zl"))
    tok = ("x", "zh", "c")
    return jax.shard_map(
        local,
        mesh=fine,
        in_specs=(P(tok, HID), P(tok, HID), P(), P(), P(HID, tok)),
        out_specs=P(tok, HID),
        check_vma=False,
    )
```

```python
import jax
import jax.numpy as jnp
from jax import lax
from jax.sharding import Mesh, PartitionSpec as P

BLOCK = 128
SIZES = {"x": 4, "zh": 4, "c": 2, "y": 4, "zl": 2}
HID = ("y", "zl")
CHUNKS = 2


def fetch(a, axis, d):
    n = SIZES[axis]
    return lax.ppermute(a, axis, [((i + d) % n, i) for i in range(n)])


def ring_gather(own, axis):
    half = own.shape[0] // 2
    ahead = fetch(own, axis, 1)
    behind = fetch(own, axis, -1)
    far = [fetch(ahead[:half], axis, 1), fetch(behind[half:], axis, -1)]
    return jnp.concatenate([own, ahead, *far, behind], axis=0)


def part(a, index, size):
    return lax.dynamic_slice_in_dim(a, index * size, size, 0)


def ring_scatter(terms, axis):
    me = lax.axis_index(axis)
    rows = terms.shape[0] // 4
    half = rows // 2
    own, ahead, far, behind = (part(terms, (me + d) % 4, rows) for d in range(4))
    to_ahead = fetch(far[:half], axis, -1)
    to_behind = fetch(far[half:], axis, 1)
    ahead = jnp.concatenate([ahead[:half] + to_ahead, ahead[half:]], axis=0)
    behind = jnp.concatenate([behind[:half], behind[half:] + to_behind], axis=0)
    return own + fetch(ahead, axis, -1) + fetch(behind, axis, 1)


def dot(a, b, dims):
    return lax.dot_general(
        a, b, (dims, ((), ())), precision=lax.Precision.HIGH, preferred_element_type=jnp.float32
    )


def local(base, source, pairs, counts, rotation):
    x, zh, c = (lax.axis_index(a) for a in ("x", "zh", "c"))
    features = rotation.shape[0] // 2
    width = rotation.shape[1]
    rows = base.shape[0]

    with jax.named_scope("core_swap_in"):
        both = jnp.concatenate([base, source], axis=0)
        low, high = both[:, :features], both[:, features:]
        mine = jnp.where(c == 0, low, high)
        theirs = fetch(jnp.where(c == 0, high, low), "c", 1)
        first = jnp.where(c == 0, mine, theirs)
        second = jnp.where(c == 0, theirs, mine)
        matrix = jnp.concatenate(
            [part(rotation, c, features), fetch(part(rotation, 1 - c, features), "c", 1)], axis=1
        )

    with jax.named_scope("gather_base"):
        chip_base = jnp.concatenate([first[:rows], second[:rows]], axis=0)
        base_all = lax.all_gather(chip_base, ("x", "zh"), axis=0, tiled=True)

    with jax.named_scope("source_terms"):
        source_terms = jnp.concatenate(
            [
                dot(ring_gather(ring_gather(own, "zh"), "x"), matrix, ((1,), (0,)))
                for own in (first[rows:], second[rows:])
            ],
            axis=0,
        )

    with jax.named_scope("base_terms"):
        base_terms = dot(base_all, matrix, ((1,), (0,)))

    tok = (x * 4 + zh) * 2
    lane = jnp.arange(width, dtype=jnp.int32)
    spot = (
        (pairs // rows) % 2 * (16 * rows)
        + (pairs // 256 - x) % 4 * (4 * rows)
        + (pairs // 64 - zh) % 4 * rows
        + pairs % rows
    ).reshape(16, CHUNKS, rows)
    limits = (counts * BLOCK).reshape(16, CHUNKS, rows)
    base_terms = base_terms.reshape(16, CHUNKS, rows, 2 * width)

    out = []
    for k in range(CHUNKS):
        with jax.named_scope(f"select_{k}"):
            taken = source_terms.at[spot[:, k].reshape(-1)].get(mode="promise_in_bounds")
            terms = base_terms[:, k].reshape(16 * rows, 2 * width)
            limit = limits[:, k].reshape(-1, 1)

            def choose(core, cols):
                return jnp.where((tok + core) * width + lane < limit, taken[:, cols], terms[:, cols])

            mixed = choose(c, slice(0, width))
            others = choose(1 - c, slice(width, 2 * width))
        with jax.named_scope(f"reduce_hid_{k}"):
            mixed = mixed + fetch(others, "c", 1)
            share = mixed.shape[0] // 4
            mixed = lax.all_to_all(mixed.reshape(4, share, width), "y", 0, 0).sum(axis=0)
            mixed = mixed + fetch(mixed, "zl", 1)
        with jax.named_scope(f"gather_hid_{k}"):
            full = lax.all_to_all(jnp.broadcast_to(mixed, (4, share, width)), "y", 0, 0)
            full = full.reshape(4 * share, width)
            full = jnp.concatenate([full, fetch(full, "c", 1)], axis=1)
        with jax.named_scope(f"inverse_{k}"):
            terms = dot(full, matrix, ((1,), (1,)))
        with jax.named_scope(f"scatter_{k}"):
            out.append(ring_scatter(ring_scatter(terms, "x"), "zh"))

    with jax.named_scope("core_swap_out"):
        mine = jnp.where(c == 0, out[0], out[1])
        theirs = fetch(jnp.where(c == 0, out[1], out[0]), "c", 1)
        return jnp.where(
            c == 0,
            jnp.concatenate([mine, theirs], axis=1),
            jnp.concatenate([theirs, mine], axis=1),
        )


def solution(mesh):
    fine = Mesh(mesh.devices.reshape(4, 4, 2, 4, 2), ("x", "zh", "c", "y", "zl"))
    tok = ("x", "zh", "c")
    return jax.shard_map(
        local,
        mesh=fine,
        in_specs=(P(tok, HID), P(tok, HID), P(), P(), P(HID, tok)),
        out_specs=P(tok, HID),
        check_vma=False,
    )
```

```python
import jax
import jax.numpy as jnp
from jax import lax
from jax.sharding import Mesh, PartitionSpec as P

BLOCK = 128
SIZES = {"x": 4, "zh": 4, "c": 2, "y": 4, "zl": 2}
HID = ("y", "zl")
RING = 640


def fetch(a, axis, d):
    n = SIZES[axis]
    return lax.ppermute(a, axis, [((i + d) % n, i) for i in range(n)])


def ring_gather(own, axis):
    half = own.shape[0] // 2
    ahead = fetch(own, axis, 1)
    behind = fetch(own, axis, -1)
    far = [fetch(ahead[:half], axis, 1), fetch(behind[half:], axis, -1)]
    return jnp.concatenate([own, ahead, *far, behind], axis=0)


def part(a, index, size):
    return lax.dynamic_slice_in_dim(a, index * size, size, 0)


def ring_scatter(terms, axis):
    me = lax.axis_index(axis)
    rows = terms.shape[0] // 4
    half = rows // 2
    own, ahead, far, behind = (part(terms, (me + d) % 4, rows) for d in range(4))
    to_ahead = fetch(far[:half], axis, -1)
    to_behind = fetch(far[half:], axis, 1)
    ahead = jnp.concatenate([ahead[:half] + to_ahead, ahead[half:]], axis=0)
    behind = jnp.concatenate([behind[:half], behind[half:] + to_behind], axis=0)
    return own + fetch(ahead, axis, -1) + fetch(behind, axis, 1)


def dot(a, b, dims):
    return lax.dot_general(
        a, b, (dims, ((), ())), precision=lax.Precision.HIGH, preferred_element_type=jnp.float32
    )


def local(base, source, pairs, counts, rotation):
    x, zh, c = (lax.axis_index(a) for a in ("x", "zh", "c"))
    features = rotation.shape[0] // 2
    width = rotation.shape[1]
    rows = base.shape[0]

    with jax.named_scope("core_swap_in"):
        both = jnp.concatenate([base, source], axis=0)
        low, high = both[:, :features], both[:, features:]
        mine = jnp.where(c == 0, low, high)
        theirs = fetch(jnp.where(c == 0, high, low), "c", 1)
        first = jnp.where(c == 0, mine, theirs)
        second = jnp.where(c == 0, theirs, mine)
        first, second, pairs, counts, rotation = lax.optimization_barrier(
            (first, second, pairs, counts, rotation)
        )
        matrix = jnp.concatenate(
            [part(rotation, c, features), fetch(part(rotation, 1 - c, features), "c", 1)], axis=1
        )

    with jax.named_scope("gather_base"):
        chip_base = jnp.concatenate([first[:rows], second[:rows]], axis=0)
        base_all = lax.all_gather(chip_base, ("x", "zh"), axis=0, tiled=True)

    with jax.named_scope("source_terms"):
        source_terms = jnp.concatenate(
            [
                dot(ring_gather(ring_gather(own, "zh"), "x"), matrix, ((1,), (0,)))
                for own in (first[rows:], second[rows:])
            ],
            axis=0,
        )

    with jax.named_scope("base_terms"):
        base_terms = dot(base_all, matrix, ((1,), (0,)))

    with jax.named_scope("select"):
        tok = (x * 4 + zh) * 2
        lane = jnp.arange(width, dtype=jnp.int32)
        columns = jnp.concatenate([(tok + c) * width + lane, (tok + 1 - c) * width + lane])
        spot = (
            (pairs // rows) % 2 * (16 * rows)
            + (pairs // 256 - x) % 4 * (4 * rows)
            + (pairs // 64 - zh) % 4 * rows
            + pairs % rows
        )
        taken = source_terms.at[spot].get(mode="promise_in_bounds")
        mixed = jnp.where(columns[None, :] < (counts * BLOCK)[:, None], taken, base_terms)

    with jax.named_scope("reduce_hid"):
        mixed = mixed[:, :width] + fetch(mixed[:, width:], "c", 1)
        share = mixed.shape[0] // 8
        mixed = lax.all_to_all(mixed.reshape(8, share, width), HID, 0, 0)
        mixed = mixed.sum(axis=0)
    with jax.named_scope("gather_hid"):
        full = lax.all_to_all(jnp.broadcast_to(mixed, (8, share, width)), HID, 0, 0)
        full = full.reshape(8 * share, width)
        other = fetch(full, "c", 1)

    with jax.named_scope("inverse"):
        full = jnp.concatenate([full, other], axis=1)
        last = dot(full, matrix[RING:], ((1,), (1,)))
        terms = dot(full, matrix[:RING], ((1,), (1,)))
    with jax.named_scope("scatter"):
        last = lax.psum_scatter(last, ("x", "zh"), scatter_dimension=0, tiled=True)
        out = ring_scatter(ring_scatter(terms, "x"), "zh")
        out = jnp.concatenate([out, last], axis=1)

    with jax.named_scope("core_swap_out"):
        mine = part(out, c, rows)
        theirs = fetch(part(out, 1 - c, rows), "c", 1)
        return jnp.where(
            c == 0,
            jnp.concatenate([mine, theirs], axis=1),
            jnp.concatenate([theirs, mine], axis=1),
        )


def solution(mesh):
    fine = Mesh(mesh.devices.reshape(4, 4, 2, 4, 2), ("x", "zh", "c", "y", "zl"))
    tok = ("x", "zh", "c")
    return jax.shard_map(
        local,
        mesh=fine,
        in_specs=(P(tok, HID), P(tok, HID), P(), P(), P(HID, tok)),
        out_specs=P(tok, HID),
        check_vma=False,
    )
```

```python
import jax
import jax.numpy as jnp
from jax import lax
from jax.sharding import Mesh, PartitionSpec as P

BLOCK = 128
SIZES = {"x": 4, "zh": 4, "c": 2, "y": 4, "zl": 2}
HID = ("y", "zl")
CHUNKS = 2


def fetch(a, axis, d):
    n = SIZES[axis]
    return lax.ppermute(a, axis, [((i + d) % n, i) for i in range(n)])


def ring_gather(own, axis):
    half = own.shape[0] // 2
    ahead = fetch(own, axis, 1)
    behind = fetch(own, axis, -1)
    far = [fetch(ahead[:half], axis, 1), fetch(behind[half:], axis, -1)]
    return jnp.concatenate([own, ahead, *far, behind], axis=0)


def part(a, index, size):
    return lax.dynamic_slice_in_dim(a, index * size, size, 0)


def far_blocks(terms, axis):
    me = lax.axis_index(axis)
    rows = terms.shape[0] // 4
    own, ahead, far, behind = (part(terms, (me + d) % 4, rows) for d in range(4))
    return own, ahead, behind, far[: rows // 2], far[rows // 2 :]


def add_far(own, ahead, behind, far_low, far_high, axis):
    half = own.shape[0] // 2
    to_ahead = fetch(far_low, axis, -1)
    to_behind = fetch(far_high, axis, 1)
    ahead = jnp.concatenate([ahead[:half] + to_ahead, ahead[half:]], axis=0)
    behind = jnp.concatenate([behind[:half], behind[half:] + to_behind], axis=0)
    return own, ahead, behind


def add_near(own, ahead, behind, axis):
    return own + fetch(ahead, axis, -1) + fetch(behind, axis, 1)


def together(*arrays):
    return lax.optimization_barrier(arrays)


def dot(a, b, dims):
    return lax.dot_general(
        a, b, (dims, ((), ())), precision=lax.Precision.HIGH, preferred_element_type=jnp.float32
    )


def local(base, source, pairs, counts, rotation):
    x, zh, c = (lax.axis_index(a) for a in ("x", "zh", "c"))
    features = rotation.shape[0] // 2
    width = rotation.shape[1]
    rows = base.shape[0]

    with jax.named_scope("core_swap_in"):
        both = jnp.concatenate([base, source], axis=0)
        low, high = both[:, :features], both[:, features:]
        mine = jnp.where(c == 0, low, high)
        theirs = fetch(jnp.where(c == 0, high, low), "c", 1)
        first = jnp.where(c == 0, mine, theirs)
        second = jnp.where(c == 0, theirs, mine)
        first, second, pairs, counts, rotation = lax.optimization_barrier(
            (first, second, pairs, counts, rotation)
        )
        matrix = jnp.concatenate(
            [part(rotation, c, features), fetch(part(rotation, 1 - c, features), "c", 1)], axis=1
        )

    with jax.named_scope("gather_base"):
        chip_base = jnp.stack([first[:rows], second[:rows]])
        base_all = lax.all_gather(chip_base, ("x", "zh"), axis=1, tiled=True)
        base_all = base_all.reshape(-1, features)

    with jax.named_scope("source_terms"):
        source_terms = jnp.concatenate(
            [
                dot(ring_gather(ring_gather(own, "zh"), "x"), matrix, ((1,), (0,)))
                for own in (first[rows:], second[rows:])
            ],
            axis=0,
        )

    with jax.named_scope("base_terms"):
        base_terms = dot(base_all, matrix, ((1,), (0,)))

    with jax.named_scope("select"):
        def by_chunk(a):
            return a.reshape(-1, CHUNKS, rows).swapaxes(0, 1).reshape(-1)

        pairs, counts = by_chunk(pairs), by_chunk(counts)
        tok = (x * 4 + zh) * 2
        lane = jnp.arange(width, dtype=jnp.int32)
        columns = jnp.concatenate([(tok + c) * width + lane, (tok + 1 - c) * width + lane])
        spot = (
            (pairs // rows) % 2 * (16 * rows)
            + (pairs // 256 - x) % 4 * (4 * rows)
            + (pairs // 64 - zh) % 4 * rows
            + pairs % rows
        )
        taken = source_terms.at[spot].get(mode="promise_in_bounds")
        mixed = jnp.where(columns[None, :] < (counts * BLOCK)[:, None], taken, base_terms)

    with jax.named_scope("reduce_hid"):
        mixed = mixed[:, :width] + fetch(mixed[:, width:], "c", 1)
        chunk = mixed.shape[0] // CHUNKS
        mixed = [mixed[:chunk], mixed[chunk:]]

    def reduce_hid(m):
        return lax.all_to_all(m.reshape(8, chunk // 8, width), HID, 0, 0).sum(axis=0)

    def gather_hid(m):
        return lax.all_to_all(jnp.broadcast_to(m, (8, *m.shape)), HID, 0, 0).reshape(chunk, width)

    def inverse(full):
        return dot(jnp.concatenate([full, fetch(full, "c", 1)], axis=1), matrix, ((1,), (1,)))

    def finish(near):
        return add_near(*add_far(*far_blocks(add_near(*near, "x"), "zh"), "zh"), "zh")

    with jax.named_scope("chunk_0"):
        full, mixed[1] = together(gather_hid(reduce_hid(mixed[0])), mixed[1])
    with jax.named_scope("chunk_1"):
        summed = reduce_hid(mixed[1])
    with jax.named_scope("chunk_0"):
        summed, *far = together(summed, *far_blocks(inverse(full), "x"))
        near = add_far(*far, "x")
    with jax.named_scope("chunk_1"):
        full, *near = together(gather_hid(summed), *near)
        near_1 = add_far(*far_blocks(inverse(full), "x"), "x")
    with jax.named_scope("scatter"):
        out = [finish(near), finish(near_1)]

    with jax.named_scope("core_swap_out"):
        mine = jnp.where(c == 0, out[0], out[1])
        theirs = fetch(jnp.where(c == 0, out[1], out[0]), "c", 1)
        return jnp.where(
            c == 0,
            jnp.concatenate([mine, theirs], axis=1),
            jnp.concatenate([theirs, mine], axis=1),
        )


def solution(mesh):
    fine = Mesh(mesh.devices.reshape(4, 4, 2, 4, 2), ("x", "zh", "c", "y", "zl"))
    tok = ("x", "zh", "c")
    return jax.shard_map(
        local,
        mesh=fine,
        in_specs=(P(tok, HID), P(tok, HID), P(), P(), P(HID, tok)),
        out_specs=P(tok, HID),
        check_vma=False,
    )
```

```python
import jax
import jax.numpy as jnp
from jax import lax
from jax.sharding import Mesh, PartitionSpec as P

BLOCK = 128
SIZES = {"x": 4, "zh": 4, "c": 2, "y": 4, "zl": 2}
HID = ("y", "zl")
CHUNKS = 2


def fetch(a, axis, d):
    n = SIZES[axis]
    return lax.ppermute(a, axis, [((i + d) % n, i) for i in range(n)])


def near_ring(own, axis):
    return own, fetch(own, axis, 1), fetch(own, axis, -1)


def far_ring(own, ahead, behind, axis):
    half = own.shape[0] // 2
    far = jnp.concatenate([fetch(ahead[:half], axis, 1), fetch(behind[half:], axis, -1)], axis=0)
    return own, ahead, far, behind


def part(a, index, size):
    return lax.dynamic_slice_in_dim(a, index * size, size, 0)


def far_blocks(terms):
    rows = terms.shape[0] // 4
    own, ahead, far, behind = (terms[d * rows : (d + 1) * rows] for d in range(4))
    return own, ahead, behind, far[: rows // 2], far[rows // 2 :]


def add_far(own, ahead, behind, far_low, far_high, axis):
    half = own.shape[0] // 2
    to_ahead = fetch(far_low, axis, -1)
    to_behind = fetch(far_high, axis, 1)
    ahead = jnp.concatenate([ahead[:half] + to_ahead, ahead[half:]], axis=0)
    behind = jnp.concatenate([behind[:half], behind[half:] + to_behind], axis=0)
    return own, ahead, behind


def add_near(own, ahead, behind, axis):
    return own + fetch(ahead, axis, -1) + fetch(behind, axis, 1)


def together(*arrays):
    return lax.optimization_barrier(arrays)


def dot(a, b, dims):
    return lax.dot_general(
        a, b, (dims, ((), ())), precision=lax.Precision.HIGH, preferred_element_type=jnp.float32
    )


def local(base, source, pairs, counts, rotation):
    x, zh, c = (lax.axis_index(a) for a in ("x", "zh", "c"))
    features = rotation.shape[0] // 2
    width = rotation.shape[1]
    rows = base.shape[0]

    with jax.named_scope("core_swap_in"):
        both = jnp.concatenate([base, source], axis=0)
        low, high = both[:, :features], both[:, features:]
        mine = jnp.where(c == 0, low, high)
        theirs = fetch(jnp.where(c == 0, high, low), "c", 1)
        first = jnp.where(c == 0, mine, theirs)
        second = jnp.where(c == 0, theirs, mine)
        first, second, rotation = together(first, second, rotation)
        matrix = jnp.concatenate(
            [part(rotation, c, features), fetch(part(rotation, 1 - c, features), "c", 1)], axis=1
        )

    with jax.named_scope("gather_tok"):
        chip_source = jnp.concatenate([first[rows:], second[rows:]], axis=0)
        base_0, base_1 = first[:rows], second[:rows]
        side = near_ring(base_1, "x")
        z_source = near_ring(chip_source, "zh")
        base_0, pairs, counts, *z_source = together(base_0, pairs, counts, *z_source)
        z_base = near_ring(base_0, "zh")
        side = jnp.concatenate(far_ring(*side, "x"), axis=0)
        z_source = jnp.concatenate(far_ring(*z_source, "zh"), axis=0)
        x_source = near_ring(z_source, "x")
        side, *z_base = together(side, *z_base)
        side = near_ring(side, "zh")
        z_base = jnp.concatenate(far_ring(*z_base, "zh"), axis=0)
        z_base, *x_source = together(z_base, *far_ring(*x_source, "x"))
        x_base = near_ring(z_base, "x")
        source_all = jnp.concatenate(x_source, axis=0)
        side = far_ring(*side, "zh")
        base_all = [
            jnp.concatenate(far_ring(*x_base, "x"), axis=0),
            jnp.concatenate([b.reshape(4, rows, features) for b in side], axis=1).reshape(-1, features),
        ]

    with jax.named_scope("source_terms"):
        source_terms = dot(source_all, matrix, ((1,), (0,)))

    with jax.named_scope("select"):

        def in_order(a):
            a = a.reshape(4, 4, CHUNKS, rows)
            a = lax.dynamic_slice_in_dim(jnp.concatenate([a, a], axis=0), x, 4, 0)
            a = lax.dynamic_slice_in_dim(jnp.concatenate([a, a], axis=1), zh, 4, 1)
            return jnp.concatenate([a[:, :, k].reshape(-1) for k in range(CHUNKS)])

        pairs, counts = in_order(pairs), in_order(counts)
        tok = (x * 4 + zh) * 2
        lane = jnp.arange(width, dtype=jnp.int32)
        columns = jnp.concatenate([(tok + c) * width + lane, (tok + 1 - c) * width + lane])
        spot = (pairs // 256 - x) % 4 * 256 + (pairs // 64 - zh) % 4 * 64 + pairs % 64
        taken = source_terms.at[spot].get(mode="promise_in_bounds")
        base_terms = jnp.concatenate([dot(b, matrix, ((1,), (0,))) for b in base_all], axis=0)
        mixed = jnp.where(columns[None, :] < (counts * BLOCK)[:, None], taken, base_terms)

    with jax.named_scope("reduce_hid"):
        mixed = mixed[:, :width] + fetch(mixed[:, width:], "c", 1)
        chunk = mixed.shape[0] // CHUNKS
        mixed = [mixed[:chunk], mixed[chunk:]]

    def reduce_hid(m):
        return lax.all_to_all(m.reshape(8, chunk // 8, width), HID, 0, 0).sum(axis=0)

    def gather_hid(m):
        return lax.all_to_all(jnp.broadcast_to(m, (8, *m.shape)), HID, 0, 0).reshape(chunk, width)

    def inverse(full):
        return dot(jnp.concatenate([full, fetch(full, "c", 1)], axis=1), matrix, ((1,), (1,)))

    def finish(near):
        return add_near(*add_far(*far_blocks(add_near(*near, "x")), "zh"), "zh")

    with jax.named_scope("chunk_0"):
        full, mixed[1] = together(gather_hid(reduce_hid(mixed[0])), mixed[1])
    with jax.named_scope("chunk_1"):
        summed = reduce_hid(mixed[1])
    with jax.named_scope("chunk_0"):
        summed, *far = together(summed, *far_blocks(inverse(full)))
        near = add_far(*far, "x")
    with jax.named_scope("chunk_1"):
        full, *near = together(gather_hid(summed), *near)
        near_1 = add_far(*far_blocks(inverse(full)), "x")
    with jax.named_scope("scatter"):
        out = [finish(near), finish(near_1)]

    with jax.named_scope("core_swap_out"):
        mine = jnp.where(c == 0, out[0], out[1])
        theirs = fetch(jnp.where(c == 0, out[1], out[0]), "c", 1)
        return jnp.where(
            c == 0,
            jnp.concatenate([mine, theirs], axis=1),
            jnp.concatenate([theirs, mine], axis=1),
        )


def solution(mesh):
    fine = Mesh(mesh.devices.reshape(4, 4, 2, 4, 2), ("x", "zh", "c", "y", "zl"))
    tok = ("x", "zh", "c")
    return jax.shard_map(
        local,
        mesh=fine,
        in_specs=(P(tok, HID), P(tok, HID), P(), P(), P(HID, tok)),
        out_specs=P(tok, HID),
        check_vma=False,
    )
```

```python
import jax
import jax.numpy as jnp
from jax import lax
from jax.experimental import pallas as pl
from jax.experimental.pallas import tpu as pltpu
from jax.sharding import Mesh, PartitionSpec as P

BLOCK = 128
SIZES = {"x": 4, "zh": 4, "c": 2, "y": 4, "zl": 2}
HID = ("y", "zl")
CHUNKS = 2


def fetch(a, axis, d):
    n = SIZES[axis]
    return lax.ppermute(a, axis, [((i + d) % n, i) for i in range(n)])


def near_ring(own, axis):
    return own, fetch(own, axis, 1), fetch(own, axis, -1)


def far_ring(own, ahead, behind, axis):
    half = own.shape[0] // 2
    return own, ahead, fetch(ahead[:half], axis, 1), fetch(behind[half:], axis, -1), behind


def part(a, index, size):
    return lax.dynamic_slice_in_dim(a, index * size, size, 0)


def far_blocks(terms, axis):
    me = lax.axis_index(axis)
    rows = terms.shape[0] // 4
    own, ahead, far, behind = (part(terms, (me + d) % 4, rows) for d in range(4))
    return own, ahead, behind, far[: rows // 2], far[rows // 2 :]


def add_far(own, ahead, behind, far_low, far_high, axis):
    half = own.shape[0] // 2
    to_ahead = fetch(far_low, axis, -1)
    to_behind = fetch(far_high, axis, 1)
    ahead = jnp.concatenate([ahead[:half] + to_ahead, ahead[half:]], axis=0)
    behind = jnp.concatenate([behind[:half], behind[half:] + to_behind], axis=0)
    return own, ahead, behind


def add_near(own, ahead, behind, axis):
    return own + fetch(ahead, axis, -1) + fetch(behind, axis, 1)


def together(*arrays):
    return lax.optimization_barrier(arrays)


def dot(a, b, dims):
    return lax.dot_general(
        a, b, (dims, ((), ())), precision=lax.Precision.HIGH, preferred_element_type=jnp.float32
    )


def halves(a):
    top = a.astype(jnp.bfloat16)
    return top, (a - top.astype(jnp.float32)).astype(jnp.bfloat16)


def split_kernel(own_ref, other_ref, top_ref, rest_ref):
    width = own_ref.shape[1]
    top_ref[:, :width], rest_ref[:, :width] = halves(own_ref[...])
    top_ref[:, width:], rest_ref[:, width:] = halves(other_ref[...])


def split_matrix(own, other):
    rows, width = own.shape
    tile = 256
    part_out = jax.ShapeDtypeStruct((rows, 2 * width), jnp.bfloat16)
    return pl.pallas_call(
        split_kernel,
        grid=(rows // tile,),
        in_specs=[pl.BlockSpec((tile, width), lambda i: (i, 0))] * 2,
        out_specs=[pl.BlockSpec((tile, 2 * width), lambda i: (i, 0))] * 2,
        out_shape=[part_out, part_out],
        cost_estimate=pl.CostEstimate(
            flops=4 * rows * width, bytes_accessed=16 * rows * width, transcendentals=0
        ),
    )(own, other)


def mix_kernel(info_ref, base_ref, top_ref, rest_ref, *refs):
    *s_refs, own_ref, other_ref, s_top, s_rest = refs

    def mul(a, b):
        return lax.dot_general(a, b, (((1,), (0,)), ((), ())), preferred_element_type=jnp.float32)

    def rotate(top, rest):
        return mul(top, top_ref[...]) + mul(rest, top_ref[...]) + mul(top, rest_ref[...])

    @pl.when(pl.program_id(0) == 0)
    def _():
        first = 0
        for ref in s_refs:
            rows = slice(first, first + ref.shape[0])
            s_top[rows], s_rest[rows] = halves(ref[...])
            first += ref.shape[0]

    tile, width = own_ref.shape
    spot = info_ref[:, 0:1]
    places = lax.broadcasted_iota(jnp.int32, (tile, s_top.shape[0]), 1)
    pick = jnp.where(places == spot, 1.0, 0.0).astype(jnp.bfloat16)
    source = rotate(mul(pick, s_top[...]).astype(jnp.bfloat16), mul(pick, s_rest[...]).astype(jnp.bfloat16))
    base = rotate(*halves(base_ref[...]))
    lane = lax.broadcasted_iota(jnp.int32, (tile, width), 1)
    own_ref[...] = jnp.where(lane < info_ref[:, 1:2], source[:, :width], base[:, :width])
    other_ref[...] = jnp.where(lane < info_ref[:, 2:3], source[:, width:], base[:, width:])


def mix(info, base, source, top, rest):
    rows, features = base.shape
    columns = top.shape[1]
    tile = 256
    out = jax.ShapeDtypeStruct((rows, columns // 2), jnp.float32)

    def whole(a):
        return pl.BlockSpec(a.shape, lambda i: (0, 0), pipeline_mode=pl.Buffered(1))

    return pl.pallas_call(
        mix_kernel,
        grid=(rows // tile,),
        in_specs=[
            pl.BlockSpec((tile, info.shape[1]), lambda i: (i, 0)),
            pl.BlockSpec((tile, features), lambda i: (i, 0)),
            *(whole(a) for a in (top, rest, *source)),
        ],
        out_specs=[pl.BlockSpec((tile, columns // 2), lambda i: (i, 0))] * 2,
        out_shape=[out, out],
        scratch_shapes=[pltpu.VMEM((rows, features), jnp.bfloat16)] * 2,
        compiler_params=pltpu.CompilerParams(vmem_limit_bytes=48 * 2**20),
        cost_estimate=pl.CostEstimate(
            flops=16 * rows * features * columns, bytes_accessed=24 * rows * features, transcendentals=0
        ),
    )(info, base, top, rest, *source)


def local(base, source, pairs, counts, rotation):
    x, zh, c = (lax.axis_index(a) for a in ("x", "zh", "c"))
    features = rotation.shape[0] // 2
    width = rotation.shape[1]
    rows = base.shape[0]

    with jax.named_scope("core_swap_in"):
        both = jnp.concatenate([base, source], axis=0)
        low, high = both[:, :features], both[:, features:]
        mine = jnp.where(c == 0, low, high)
        theirs = fetch(jnp.where(c == 0, high, low), "c", 1)
        first = jnp.where(c == 0, mine, theirs)
        second = jnp.where(c == 0, theirs, mine)
        first, second, pairs, counts, rotation = lax.optimization_barrier(
            (first, second, pairs, counts, rotation)
        )
        mine = part(rotation, c, features)
        theirs = fetch(part(rotation, 1 - c, features), "c", 1)
        matrix = jnp.concatenate([mine, theirs], axis=1)
        top, rest = split_matrix(mine, theirs)

    with jax.named_scope("gather_base"):
        chip_base = jnp.stack([first[:rows], second[:rows]])
        base_all = lax.all_gather(chip_base, ("x", "zh"), axis=1, tiled=True)
        base_all = base_all.reshape(-1, features)

    with jax.named_scope("gather_source"):
        near = [
            near_ring(jnp.concatenate(far_ring(*near_ring(own, "zh"), "zh"), axis=0), "x")
            for own in (first[rows:], second[rows:])
        ]
        top, rest, *near[1] = together(top, rest, *near[1])
        source_all = [piece for n in near for piece in far_ring(*n, "x")]

    with jax.named_scope("select"):
        def by_chunk(a):
            return a.reshape(-1, CHUNKS, rows).swapaxes(0, 1).reshape(-1)

        pairs, counts = by_chunk(pairs), by_chunk(counts)
        tok = (x * 4 + zh) * 2
        spot = (
            (pairs // rows) % 2 * (16 * rows)
            + (pairs // 256 - x) % 4 * (4 * rows)
            + (pairs // 64 - zh) % 4 * rows
            + pairs % rows
        )
        limits = counts * BLOCK
        info = jnp.stack(
            [spot, limits - (tok + c) * width, limits - (tok + 1 - c) * width, spot], axis=1
        )
        mixed, others = mix(info, base_all, source_all, top, rest)

    with jax.named_scope("reduce_hid"):
        mixed = mixed + fetch(others, "c", 1)
        chunk = mixed.shape[0] // CHUNKS
        mixed = [mixed[:chunk], mixed[chunk:]]

    def reduce_hid(m):
        return lax.all_to_all(m.reshape(8, chunk // 8, width), HID, 0, 0).sum(axis=0)

    def gather_hid(m):
        return lax.all_to_all(jnp.broadcast_to(m, (8, *m.shape)), HID, 0, 0).reshape(chunk, width)

    def inverse(full):
        return dot(jnp.concatenate([full, fetch(full, "c", 1)], axis=1), matrix, ((1,), (1,)))

    def finish(near):
        return add_near(*add_far(*far_blocks(add_near(*near, "x"), "zh"), "zh"), "zh")

    with jax.named_scope("chunk_0"):
        full, mixed[1] = together(gather_hid(reduce_hid(mixed[0])), mixed[1])
    with jax.named_scope("chunk_1"):
        summed = reduce_hid(mixed[1])
    with jax.named_scope("chunk_0"):
        summed, *far = together(summed, *far_blocks(inverse(full), "x"))
        near = add_far(*far, "x")
    with jax.named_scope("chunk_1"):
        full, *near = together(gather_hid(summed), *near)
        near_1 = add_far(*far_blocks(inverse(full), "x"), "x")
    with jax.named_scope("scatter"):
        out = [finish(near), finish(near_1)]

    with jax.named_scope("core_swap_out"):
        mine = jnp.where(c == 0, out[0], out[1])
        theirs = fetch(jnp.where(c == 0, out[1], out[0]), "c", 1)
        return jnp.where(
            c == 0,
            jnp.concatenate([mine, theirs], axis=1),
            jnp.concatenate([theirs, mine], axis=1),
        )


def solution(mesh):
    fine = Mesh(mesh.devices.reshape(4, 4, 2, 4, 2), ("x", "zh", "c", "y", "zl"))
    tok = ("x", "zh", "c")
    return jax.shard_map(
        local,
        mesh=fine,
        in_specs=(P(tok, HID), P(tok, HID), P(), P(), P(HID, tok)),
        out_specs=P(tok, HID),
        check_vma=False,
    )
```

```python
import jax
import jax.numpy as jnp
from jax import lax
from jax.experimental import pallas as pl
from jax.experimental.pallas import tpu as pltpu
from jax.sharding import Mesh, PartitionSpec as P

BLOCK = 128
SIZES = {"x": 4, "zh": 4, "c": 2, "y": 4, "zl": 2}
HID = ("y", "zl")
CHUNKS = 2


def fetch(a, axis, d):
    n = SIZES[axis]
    return lax.ppermute(a, axis, [((i + d) % n, i) for i in range(n)])


def near_ring(own, axis):
    return own, fetch(own, axis, 1), fetch(own, axis, -1)


def far_ring(own, ahead, behind, axis):
    half = own.shape[0] // 2
    return own, ahead, fetch(ahead[:half], axis, 1), fetch(behind[half:], axis, -1), behind


def part(a, index, size):
    return lax.dynamic_slice_in_dim(a, index * size, size, 0)


def far_blocks(terms, axis):
    me = lax.axis_index(axis)
    rows = terms.shape[0] // 4
    own, ahead, far, behind = (part(terms, (me + d) % 4, rows) for d in range(4))
    return own, ahead, behind, far[: rows // 2], far[rows // 2 :]


def add_far(own, ahead, behind, far_low, far_high, axis):
    half = own.shape[0] // 2
    to_ahead = fetch(far_low, axis, -1)
    to_behind = fetch(far_high, axis, 1)
    ahead = jnp.concatenate([ahead[:half] + to_ahead, ahead[half:]], axis=0)
    behind = jnp.concatenate([behind[:half], behind[half:] + to_behind], axis=0)
    return own, ahead, behind


def add_near(own, ahead, behind, axis):
    return own + fetch(ahead, axis, -1) + fetch(behind, axis, 1)


def together(*arrays):
    return lax.optimization_barrier(arrays)


def dot(a, b, dims):
    return lax.dot_general(
        a, b, (dims, ((), ())), precision=lax.Precision.HIGH, preferred_element_type=jnp.float32
    )


def halves(a):
    top = a.astype(jnp.bfloat16)
    return top, (a - top.astype(jnp.float32)).astype(jnp.bfloat16)


def split_kernel(core_ref, own_ref, other_ref, full_ref, top_ref, rest_ref):
    width = own_ref.shape[1]
    for ref, columns in ((own_ref, slice(0, width)), (other_ref, slice(width, 2 * width))):
        full_ref[:, columns] = ref[...]
        top_ref[:, columns], rest_ref[:, columns] = halves(ref[...])


def split_matrix(core, rotation, other):
    rows, width = other.shape
    tile = 256
    steps = rows // tile
    shape = (rows, 2 * width)
    return pl.pallas_call(
        split_kernel,
        grid_spec=pltpu.PrefetchScalarGridSpec(
            num_scalar_prefetch=1,
            grid=(steps,),
            in_specs=[
                pl.BlockSpec((tile, width), lambda i, core: (core[0] * steps + i, 0)),
                pl.BlockSpec((tile, width), lambda i, core: (i, 0)),
            ],
            out_specs=[pl.BlockSpec((tile, 2 * width), lambda i, core: (i, 0))] * 3,
        ),
        out_shape=[
            jax.ShapeDtypeStruct(shape, jnp.float32),
            jax.ShapeDtypeStruct(shape, jnp.bfloat16),
            jax.ShapeDtypeStruct(shape, jnp.bfloat16),
        ],
        cost_estimate=pl.CostEstimate(
            flops=4 * rows * width, bytes_accessed=24 * rows * width, transcendentals=0
        ),
    )(core.reshape(1), rotation, other)


def mix_kernel(info_ref, base_ref, top_ref, rest_ref, *refs):
    *s_refs, own_ref, other_ref, s_top, s_rest = refs

    def mul(a, b):
        return lax.dot_general(a, b, (((1,), (0,)), ((), ())), preferred_element_type=jnp.float32)

    def rotate(top, rest):
        return mul(top, top_ref[...]) + mul(rest, top_ref[...]) + mul(top, rest_ref[...])

    @pl.when(pl.program_id(0) == 0)
    def _():
        first = 0
        for ref in s_refs:
            rows = slice(first, first + ref.shape[0])
            s_top[rows], s_rest[rows] = halves(ref[...])
            first += ref.shape[0]

    tile, width = own_ref.shape
    spot = info_ref[:, 0:1]
    places = lax.broadcasted_iota(jnp.int32, (tile, s_top.shape[0]), 1)
    pick = jnp.where(places == spot, 1.0, 0.0).astype(jnp.bfloat16)
    source = rotate(mul(pick, s_top[...]).astype(jnp.bfloat16), mul(pick, s_rest[...]).astype(jnp.bfloat16))
    base = rotate(*halves(base_ref[...]))
    lane = lax.broadcasted_iota(jnp.int32, (tile, width), 1)
    own_ref[...] = jnp.where(lane < info_ref[:, 1:2], source[:, :width], base[:, :width])
    other_ref[...] = jnp.where(lane < info_ref[:, 2:3], source[:, width:], base[:, width:])


def mix(chunk, info, base, source, top, rest):
    features = base.shape[1]
    rows = base.shape[0] // CHUNKS
    columns = top.shape[1]
    tile = 256
    steps = rows // tile
    out = jax.ShapeDtypeStruct((rows, columns // 2), jnp.float32)

    def whole(a):
        return pl.BlockSpec(a.shape, lambda i: (0, 0), pipeline_mode=pl.Buffered(1))

    return pl.pallas_call(
        mix_kernel,
        grid=(steps,),
        in_specs=[
            pl.BlockSpec((tile, info.shape[1]), lambda i: (chunk * steps + i, 0)),
            pl.BlockSpec((tile, features), lambda i: (chunk * steps + i, 0)),
            *(whole(a) for a in (top, rest, *source)),
        ],
        out_specs=[pl.BlockSpec((tile, columns // 2), lambda i: (i, 0))] * 2,
        out_shape=[out, out],
        scratch_shapes=[pltpu.VMEM((CHUNKS * rows, features), jnp.bfloat16)] * 2,
        compiler_params=pltpu.CompilerParams(vmem_limit_bytes=48 * 2**20),
        cost_estimate=pl.CostEstimate(
            flops=16 * rows * features * columns, bytes_accessed=24 * rows * features, transcendentals=0
        ),
    )(info, base, top, rest, *source)


def local(base, source, pairs, counts, rotation):
    x, zh, c = (lax.axis_index(a) for a in ("x", "zh", "c"))
    features = rotation.shape[0] // 2
    width = rotation.shape[1]
    rows = base.shape[0]

    with jax.named_scope("core_swap_in"):
        both = jnp.concatenate([base, source], axis=0)
        low, high = both[:, :features], both[:, features:]
        mine = jnp.where(c == 0, low, high)
        theirs = fetch(jnp.where(c == 0, high, low), "c", 1)
        first = jnp.where(c == 0, mine, theirs)
        second = jnp.where(c == 0, theirs, mine)
        first, second, pairs, counts = together(first, second, pairs, counts)

    with jax.named_scope("gather_base"):
        chip_base = jnp.stack([first[:rows], second[:rows]])
        base_all = lax.all_gather(chip_base, ("x", "zh"), axis=1, tiled=True)
        base_all = base_all.reshape(-1, features)

    with jax.named_scope("gather_source"):
        near = [near_ring(own, "zh") for own in (first[rows:], second[rows:])]
        rotation, *near = together(rotation, *near[0], *near[1])
        near = [near[:3], near[3:]]
        near = [near_ring(jnp.concatenate(far_ring(*n, "zh"), axis=0), "x") for n in near]
        theirs = fetch(part(rotation, 1 - c, features), "c", 1)
        matrix, top, rest = split_matrix(c, rotation, theirs)
        top, rest, *near[1] = together(top, rest, *near[1])
        source_all = [piece for n in near for piece in far_ring(*n, "x")]

    with jax.named_scope("select"):
        def by_chunk(a):
            return a.reshape(-1, CHUNKS, rows).swapaxes(0, 1).reshape(-1)

        pairs, counts = by_chunk(pairs), by_chunk(counts)
        tok = (x * 4 + zh) * 2
        spot = (
            (pairs // rows) % 2 * (16 * rows)
            + (pairs // 256 - x) % 4 * (4 * rows)
            + (pairs // 64 - zh) % 4 * rows
            + pairs % rows
        )
        limits = counts * BLOCK
        info = jnp.stack(
            [spot, limits - (tok + c) * width, limits - (tok + 1 - c) * width, spot], axis=1
        )

    def mix_chunk(k, base_all):
        mixed, others = mix(k, info, base_all, source_all, top, rest)
        return mixed + fetch(others, "c", 1)

    chunk = base_all.shape[0] // CHUNKS

    def reduce_hid(m):
        return lax.all_to_all(m.reshape(8, chunk // 8, width), HID, 0, 0).sum(axis=0)

    def gather_hid(m):
        return lax.all_to_all(jnp.broadcast_to(m, (8, *m.shape)), HID, 0, 0).reshape(chunk, width)

    def inverse(full):
        return dot(jnp.concatenate([full, fetch(full, "c", 1)], axis=1), matrix, ((1,), (1,)))

    def finish(near):
        return add_near(*add_far(*far_blocks(add_near(*near, "x"), "zh"), "zh"), "zh")

    with jax.named_scope("chunk_0"):
        mixed, base_all = together(mix_chunk(0, base_all), base_all)
        summed = reduce_hid(mixed)
    with jax.named_scope("mix_1"):
        mixed, summed = together(mix_chunk(1, base_all), summed)
    with jax.named_scope("chunk_0"):
        full, mixed = together(gather_hid(summed), mixed)
    with jax.named_scope("chunk_1"):
        summed = reduce_hid(mixed)
    with jax.named_scope("chunk_0"):
        summed, *far = together(summed, *far_blocks(inverse(full), "x"))
        near = add_far(*far, "x")
    with jax.named_scope("chunk_1"):
        full, *near = together(gather_hid(summed), *near)
        near_1 = add_far(*far_blocks(inverse(full), "x"), "x")
    with jax.named_scope("scatter"):
        out = [finish(near), finish(near_1)]

    with jax.named_scope("core_swap_out"):
        mine = jnp.where(c == 0, out[0], out[1])
        theirs = fetch(jnp.where(c == 0, out[1], out[0]), "c", 1)
        return jnp.where(
            c == 0,
            jnp.concatenate([mine, theirs], axis=1),
            jnp.concatenate([theirs, mine], axis=1),
        )


def solution(mesh):
    fine = Mesh(mesh.devices.reshape(4, 4, 2, 4, 2), ("x", "zh", "c", "y", "zl"))
    tok = ("x", "zh", "c")
    return jax.shard_map(
        local,
        mesh=fine,
        in_specs=(P(tok, HID), P(tok, HID), P(), P(), P(HID, tok)),
        out_specs=P(tok, HID),
        check_vma=False,
    )
```

```python
import jax
import jax.numpy as jnp
from jax import lax
from jax.experimental import pallas as pl
from jax.experimental.pallas import tpu as pltpu
from jax.sharding import Mesh, PartitionSpec as P

BLOCK = 128
SIZES = {"x": 4, "zh": 4, "c": 2, "y": 4, "zl": 2}
HID = ("y", "zl")
CHUNKS = 2


def fetch(a, axis, d):
    n = SIZES[axis]
    return lax.ppermute(a, axis, [((i + d) % n, i) for i in range(n)])


def near_ring(own, axis):
    return own, fetch(own, axis, 1), fetch(own, axis, -1)


def far_ring(own, ahead, behind, axis):
    half = own.shape[0] // 2
    return own, ahead, fetch(ahead[:half], axis, 1), fetch(behind[half:], axis, -1), behind


def part(a, index, size):
    return lax.dynamic_slice_in_dim(a, index * size, size, 0)


def far_blocks(terms, axis):
    me = lax.axis_index(axis)
    rows = terms.shape[0] // 4
    own, ahead, far, behind = (part(terms, (me + d) % 4, rows) for d in range(4))
    return own, ahead, behind, far[: rows // 2], far[rows // 2 :]


def add_far(own, ahead, behind, far_low, far_high, axis):
    half = own.shape[0] // 2
    to_ahead = fetch(far_low, axis, -1)
    to_behind = fetch(far_high, axis, 1)
    ahead = jnp.concatenate([ahead[:half] + to_ahead, ahead[half:]], axis=0)
    behind = jnp.concatenate([behind[:half], behind[half:] + to_behind], axis=0)
    return own, ahead, behind


def add_near(own, ahead, behind, axis):
    return own + fetch(ahead, axis, -1) + fetch(behind, axis, 1)


def together(*arrays):
    return lax.optimization_barrier(arrays)


def dot(a, b, dims):
    return lax.dot_general(
        a, b, (dims, ((), ())), precision=lax.Precision.HIGH, preferred_element_type=jnp.float32
    )


def halves(a):
    top = a.astype(jnp.bfloat16)
    return top, (a - top.astype(jnp.float32)).astype(jnp.bfloat16)


def split_kernel(core_ref, own_ref, other_ref, full_ref, top_ref, rest_ref):
    width = own_ref.shape[1]
    for ref, columns in ((own_ref, slice(0, width)), (other_ref, slice(width, 2 * width))):
        full_ref[:, columns] = ref[...]
        top_ref[:, columns], rest_ref[:, columns] = halves(ref[...])


def split_matrix(core, rotation, other):
    rows, width = other.shape
    tile = 256
    steps = rows // tile
    shape = (rows, 2 * width)
    return pl.pallas_call(
        split_kernel,
        grid_spec=pltpu.PrefetchScalarGridSpec(
            num_scalar_prefetch=1,
            grid=(steps,),
            in_specs=[
                pl.BlockSpec((tile, width), lambda i, core: (core[0] * steps + i, 0)),
                pl.BlockSpec((tile, width), lambda i, core: (i, 0)),
            ],
            out_specs=[pl.BlockSpec((tile, 2 * width), lambda i, core: (i, 0))] * 3,
        ),
        out_shape=[
            jax.ShapeDtypeStruct(shape, jnp.float32),
            jax.ShapeDtypeStruct(shape, jnp.bfloat16),
            jax.ShapeDtypeStruct(shape, jnp.bfloat16),
        ],
        cost_estimate=pl.CostEstimate(
            flops=4 * rows * width, bytes_accessed=24 * rows * width, transcendentals=0
        ),
    )(core.reshape(1), rotation, other)


def mix_kernel(info_ref, base_ref, top_ref, rest_ref, *refs):
    *s_refs, own_ref, other_ref, s_top, s_rest = refs

    def mul(a, b):
        return lax.dot_general(a, b, (((1,), (0,)), ((), ())), preferred_element_type=jnp.float32)

    def rotate(top, rest):
        return mul(top, top_ref[...]) + mul(rest, top_ref[...]) + mul(top, rest_ref[...])

    @pl.when(pl.program_id(0) == 0)
    def _():
        first = 0
        for ref in s_refs:
            rows = slice(first, first + ref.shape[0])
            s_top[rows], s_rest[rows] = halves(ref[...])
            first += ref.shape[0]

    tile, width = own_ref.shape
    spot = info_ref[:, 0:1]
    places = lax.broadcasted_iota(jnp.int32, (tile, s_top.shape[0]), 1)
    pick = jnp.where(places == spot, 1.0, 0.0).astype(jnp.bfloat16)
    source = rotate(mul(pick, s_top[...]).astype(jnp.bfloat16), mul(pick, s_rest[...]).astype(jnp.bfloat16))
    base = rotate(*halves(base_ref[...]))
    lane = lax.broadcasted_iota(jnp.int32, (tile, width), 1)
    own_ref[...] = jnp.where(lane < info_ref[:, 1:2], source[:, :width], base[:, :width])
    other_ref[...] = jnp.where(lane < info_ref[:, 2:3], source[:, width:], base[:, width:])


def mix(chunk, info, base, source, top, rest):
    features = base.shape[1]
    rows = base.shape[0] // CHUNKS
    columns = top.shape[1]
    tile = 256
    steps = rows // tile
    out = jax.ShapeDtypeStruct((rows, columns // 2), jnp.float32)

    def whole(a):
        return pl.BlockSpec(a.shape, lambda i: (0, 0), pipeline_mode=pl.Buffered(1))

    return pl.pallas_call(
        mix_kernel,
        grid=(steps,),
        in_specs=[
            pl.BlockSpec((tile, info.shape[1]), lambda i: (chunk * steps + i, 0)),
            pl.BlockSpec((tile, features), lambda i: (chunk * steps + i, 0)),
            *(whole(a) for a in (top, rest, *source)),
        ],
        out_specs=[pl.BlockSpec((tile, columns // 2), lambda i: (i, 0))] * 2,
        out_shape=[out, out],
        scratch_shapes=[pltpu.VMEM((CHUNKS * rows, features), jnp.bfloat16)] * 2,
        compiler_params=pltpu.CompilerParams(vmem_limit_bytes=48 * 2**20),
        cost_estimate=pl.CostEstimate(
            flops=16 * rows * features * columns, bytes_accessed=24 * rows * features, transcendentals=0
        ),
    )(info, base, top, rest, *source)


def local(base, source, pairs, counts, rotation):
    x, zh, c = (lax.axis_index(a) for a in ("x", "zh", "c"))
    features = rotation.shape[0] // 2
    width = rotation.shape[1]
    rows = base.shape[0]

    with jax.named_scope("core_swap_in"):

        def pick(core):
            picked = [jnp.where(core == 0, a[:, :features], a[:, features:]) for a in (base, source)]
            return jnp.concatenate(picked, axis=0)

        mine = pick(c)
        theirs = fetch(pick(1 - c), "c", 1)
        first = jnp.where(c == 0, mine, theirs)
        second = jnp.where(c == 0, theirs, mine)
        first, second, pairs, counts = together(first, second, pairs, counts)

    with jax.named_scope("gather_base"):
        chip_base = jnp.stack([first[:rows], second[:rows]])
        base_all = lax.all_gather(chip_base, ("x", "zh"), axis=1, tiled=True)
        base_all = base_all.reshape(-1, features)

    with jax.named_scope("gather_source"):
        near = [near_ring(own, "zh") for own in (first[rows:], second[rows:])]
        rotation, *near = together(rotation, *near[0], *near[1])
        near = [near[:3], near[3:]]
        near = [near_ring(jnp.concatenate(far_ring(*n, "zh"), axis=0), "x") for n in near]
        theirs = fetch(part(rotation, 1 - c, features), "c", 1)
        matrix, top, rest = split_matrix(c, rotation, theirs)
        top, rest, *near[1] = together(top, rest, *near[1])
        source_all = [piece for n in near for piece in far_ring(*n, "x")]

    with jax.named_scope("select"):
        def by_chunk(a):
            return a.reshape(-1, CHUNKS, rows).swapaxes(0, 1).reshape(-1)

        pairs, counts = by_chunk(pairs), by_chunk(counts)
        tok = (x * 4 + zh) * 2
        spot = (
            (pairs // rows) % 2 * (16 * rows)
            + (pairs // 256 - x) % 4 * (4 * rows)
            + (pairs // 64 - zh) % 4 * rows
            + pairs % rows
        )
        limits = counts * BLOCK
        info = jnp.stack(
            [spot, limits - (tok + c) * width, limits - (tok + 1 - c) * width, spot], axis=1
        )

    def mix_chunk(k, base_all):
        mixed, others = mix(k, info, base_all, source_all, top, rest)
        return mixed + fetch(others, "c", 1)

    chunk = base_all.shape[0] // CHUNKS

    def reduce_hid(m):
        return lax.all_to_all(m.reshape(8, chunk // 8, width), HID, 0, 0).sum(axis=0)

    def gather_hid(m):
        return lax.all_to_all(jnp.broadcast_to(m, (8, *m.shape)), HID, 0, 0).reshape(chunk, width)

    def inverse(full):
        return dot(jnp.concatenate([full, fetch(full, "c", 1)], axis=1), matrix, ((1,), (1,)))

    def finish(near):
        return add_near(*add_far(*far_blocks(add_near(*near, "x"), "zh"), "zh"), "zh")

    with jax.named_scope("chunk_0"):
        mixed, base_all = together(mix_chunk(0, base_all), base_all)
        summed = reduce_hid(mixed)
    with jax.named_scope("mix_1"):
        mixed, summed = together(mix_chunk(1, base_all), summed)
    with jax.named_scope("both_chunks"):
        share = chunk // 8
        sent = jnp.concatenate(
            [mixed.reshape(8, share, width), jnp.broadcast_to(summed, (8, share, width))], axis=1
        )
        got = lax.all_to_all(sent, HID, 0, 0)
        summed = got[:, :share].sum(axis=0)
        full = got[:, share:].reshape(chunk, width)
    with jax.named_scope("chunk_0"):
        near = add_far(*together(*far_blocks(inverse(full), "x")), "x")
    with jax.named_scope("chunk_1"):
        full, *near = together(gather_hid(summed), *near)
        near_1 = add_far(*together(*far_blocks(inverse(full), "x")), "x")
    with jax.named_scope("scatter"):
        out = [finish(near), finish(near_1)]

    with jax.named_scope("core_swap_out"):
        mine = jnp.where(c == 0, out[0], out[1])
        theirs = fetch(jnp.where(c == 0, out[1], out[0]), "c", 1)
        return jnp.where(
            c == 0,
            jnp.concatenate([mine, theirs], axis=1),
            jnp.concatenate([theirs, mine], axis=1),
        )


def solution(mesh):
    fine = Mesh(mesh.devices.reshape(4, 4, 2, 4, 2), ("x", "zh", "c", "y", "zl"))
    tok = ("x", "zh", "c")
    return jax.shard_map(
        local,
        mesh=fine,
        in_specs=(P(tok, HID), P(tok, HID), P(), P(), P(HID, tok)),
        out_specs=P(tok, HID),
        check_vma=False,
    )
```

```python
import jax
import jax.numpy as jnp
from jax import lax
from jax.experimental import pallas as pl
from jax.experimental.pallas import tpu as pltpu
from jax.sharding import Mesh, PartitionSpec as P

BLOCK = 128
SIZES = {"x": 4, "zh": 4, "c": 2, "y": 4, "zl": 2}
HID = ("y", "zl")
CHUNKS = 2


def fetch(a, axis, d):
    n = SIZES[axis]
    return lax.ppermute(a, axis, [((i + d) % n, i) for i in range(n)])


def near_ring(own, axis):
    return own, fetch(own, axis, 1), fetch(own, axis, -1)


def far_ring(own, ahead, behind, axis):
    half = own.shape[0] // 2
    return own, ahead, fetch(ahead[:half], axis, 1), fetch(behind[half:], axis, -1), behind


def part(a, index, size):
    return lax.dynamic_slice_in_dim(a, index * size, size, 0)


def far_blocks(terms, axis):
    me = lax.axis_index(axis)
    rows = terms.shape[0] // 4
    own, ahead, far, behind = (part(terms, (me + d) % 4, rows) for d in range(4))
    return own, ahead, behind, far[: rows // 2], far[rows // 2 :]


def add_far(own, ahead, behind, far_low, far_high, axis):
    half = own.shape[0] // 2
    to_ahead = fetch(far_low, axis, -1)
    to_behind = fetch(far_high, axis, 1)
    ahead = jnp.concatenate([ahead[:half] + to_ahead, ahead[half:]], axis=0)
    behind = jnp.concatenate([behind[:half], behind[half:] + to_behind], axis=0)
    return own, ahead, behind


def add_near(own, ahead, behind, axis):
    return own + fetch(ahead, axis, -1) + fetch(behind, axis, 1)


def together(*arrays):
    return lax.optimization_barrier(arrays)


def dot(a, b, dims):
    return lax.dot_general(
        a, b, (dims, ((), ())), precision=lax.Precision.HIGH, preferred_element_type=jnp.float32
    )


def halves(a):
    top = a.astype(jnp.bfloat16)
    return top, (a - top.astype(jnp.float32)).astype(jnp.bfloat16)


def split_kernel(core_ref, own_ref, other_ref, full_ref, top_ref, rest_ref):
    width = own_ref.shape[1]
    for ref, columns in ((own_ref, slice(0, width)), (other_ref, slice(width, 2 * width))):
        full_ref[:, columns] = ref[...]
        top_ref[:, columns], rest_ref[:, columns] = halves(ref[...])


def split_matrix(core, rotation, other):
    rows, width = other.shape[0] // 2, other.shape[1]
    tile = 256
    steps = rows // tile
    shape = (rows, 2 * width)
    return pl.pallas_call(
        split_kernel,
        grid_spec=pltpu.PrefetchScalarGridSpec(
            num_scalar_prefetch=1,
            grid=(steps,),
            in_specs=[pl.BlockSpec((tile, width), lambda i, core: (core[0] * steps + i, 0))] * 2,
            out_specs=[pl.BlockSpec((tile, 2 * width), lambda i, core: (i, 0))] * 3,
        ),
        out_shape=[
            jax.ShapeDtypeStruct(shape, jnp.float32),
            jax.ShapeDtypeStruct(shape, jnp.bfloat16),
            jax.ShapeDtypeStruct(shape, jnp.bfloat16),
        ],
        cost_estimate=pl.CostEstimate(
            flops=4 * rows * width, bytes_accessed=24 * rows * width, transcendentals=0
        ),
    )(core.reshape(1), rotation, other)


def mix_kernel(info_ref, base_ref, top_ref, rest_ref, *refs):
    *s_refs, own_ref, other_ref, s_top, s_rest = refs

    def mul(a, b):
        return lax.dot_general(a, b, (((1,), (0,)), ((), ())), preferred_element_type=jnp.float32)

    def rotate(top, rest):
        return mul(top, top_ref[...]) + mul(rest, top_ref[...]) + mul(top, rest_ref[...])

    @pl.when(pl.program_id(0) == 0)
    def _():
        first = 0
        for ref in s_refs:
            rows = slice(first, first + ref.shape[0])
            s_top[rows], s_rest[rows] = halves(ref[...])
            first += ref.shape[0]

    tile, width = own_ref.shape
    spot = info_ref[:, 0:1]
    places = lax.broadcasted_iota(jnp.int32, (tile, s_top.shape[0]), 1)
    pick = jnp.where(places == spot, 1.0, 0.0).astype(jnp.bfloat16)
    source = rotate(mul(pick, s_top[...]).astype(jnp.bfloat16), mul(pick, s_rest[...]).astype(jnp.bfloat16))
    base = rotate(*halves(base_ref[...]))
    lane = lax.broadcasted_iota(jnp.int32, (tile, width), 1)
    own_ref[...] = jnp.where(lane < info_ref[:, 1:2], source[:, :width], base[:, :width])
    other_ref[...] = jnp.where(lane < info_ref[:, 2:3], source[:, width:], base[:, width:])


def mix(chunk, info, base, source, top, rest):
    features = base.shape[1]
    rows = base.shape[0] // CHUNKS
    columns = top.shape[1]
    tile = 256
    steps = rows // tile
    out = jax.ShapeDtypeStruct((rows, columns // 2), jnp.float32)

    def whole(a):
        return pl.BlockSpec(a.shape, lambda i: (0, 0), pipeline_mode=pl.Buffered(1))

    return pl.pallas_call(
        mix_kernel,
        grid=(steps,),
        in_specs=[
            pl.BlockSpec((tile, info.shape[1]), lambda i: (chunk * steps + i, 0)),
            pl.BlockSpec((tile, features), lambda i: (chunk * steps + i, 0)),
            *(whole(a) for a in (top, rest, *source)),
        ],
        out_specs=[pl.BlockSpec((tile, columns // 2), lambda i: (i, 0))] * 2,
        out_shape=[out, out],
        scratch_shapes=[pltpu.VMEM((CHUNKS * rows, features), jnp.bfloat16)] * 2,
        compiler_params=pltpu.CompilerParams(vmem_limit_bytes=48 * 2**20),
        cost_estimate=pl.CostEstimate(
            flops=16 * rows * features * columns, bytes_accessed=24 * rows * features, transcendentals=0
        ),
    )(info, base, top, rest, *source)


def local(base, source, pairs, counts, rotation):
    x, zh, c = (lax.axis_index(a) for a in ("x", "zh", "c"))
    features = rotation.shape[0] // 2
    width = rotation.shape[1]
    rows = base.shape[0]

    with jax.named_scope("core_swap_in"):

        def pick(core):
            picked = [jnp.where(core == 0, a[:, :features], a[:, features:]) for a in (base, source)]
            return jnp.concatenate(picked, axis=0)

        mine = pick(c)
        theirs = fetch(pick(1 - c), "c", 1)
        first = jnp.where(c == 0, mine, theirs)
        second = jnp.where(c == 0, theirs, mine)
        first, second, pairs, counts, rotation = together(first, second, pairs, counts, rotation)

    with jax.named_scope("gather_base"):
        chip_base = jnp.stack([first[:rows], second[:rows]])
        base_all = lax.all_gather(chip_base, ("x", "zh"), axis=1, tiled=True)
        base_all = base_all.reshape(-1, features)

    with jax.named_scope("gather_source"):
        near = [near_ring(own, "zh") for own in (first[rows:], second[rows:])]
        near = [near_ring(jnp.concatenate(far_ring(*n, "zh"), axis=0), "x") for n in near]
        matrix, top, rest = split_matrix(c, rotation, fetch(rotation, "c", 1))
        top, rest, *near[1] = together(top, rest, *near[1])
        source_all = [piece for n in near for piece in far_ring(*n, "x")]

    with jax.named_scope("select"):
        def by_chunk(a):
            return a.reshape(-1, CHUNKS, rows).swapaxes(0, 1).reshape(-1)

        pairs, counts = by_chunk(pairs), by_chunk(counts)
        tok = (x * 4 + zh) * 2
        spot = (
            (pairs // rows) % 2 * (16 * rows)
            + (pairs // 256 - x) % 4 * (4 * rows)
            + (pairs // 64 - zh) % 4 * rows
            + pairs % rows
        )
        limits = counts * BLOCK
        info = jnp.stack(
            [spot, limits - (tok + c) * width, limits - (tok + 1 - c) * width, spot], axis=1
        )

    def mix_chunk(k, base_all):
        mixed, others = mix(k, info, base_all, source_all, top, rest)
        return mixed + fetch(others, "c", 1)

    chunk = base_all.shape[0] // CHUNKS

    def reduce_hid(m):
        return lax.all_to_all(m.reshape(8, chunk // 8, width), HID, 0, 0).sum(axis=0)

    def gather_hid(m):
        return lax.all_to_all(jnp.broadcast_to(m, (8, *m.shape)), HID, 0, 0).reshape(chunk, width)

    def inverse(full):
        return dot(jnp.concatenate([full, fetch(full, "c", 1)], axis=1), matrix, ((1,), (1,)))

    def finish_ring(near):
        return add_near(*add_far(*far_blocks(add_near(*near, "x"), "zh"), "zh"), "zh")

    def finish_direct(near):
        terms = add_near(*near, "x")
        own, *others = (part(terms, (zh + d) % 4, rows) for d in range(4))
        return own + sum(fetch(a, "zh", -d) for d, a in enumerate(others, 1))

    with jax.named_scope("chunk_0"):
        mixed, base_all = together(mix_chunk(0, base_all), base_all)
        summed = reduce_hid(mixed)
    with jax.named_scope("mix_1"):
        mixed, summed = together(mix_chunk(1, base_all), summed)
    with jax.named_scope("both_chunks"):
        share = chunk // 8
        sent = jnp.concatenate(
            [mixed.reshape(8, share, width), jnp.broadcast_to(summed, (8, share, width))], axis=1
        )
        got = lax.all_to_all(sent, HID, 0, 0)
        summed = got[:, :share].sum(axis=0)
        full = got[:, share:].reshape(chunk, width)
    with jax.named_scope("chunk_0"):
        near = add_far(*together(*far_blocks(inverse(full), "x")), "x")
    with jax.named_scope("chunk_1"):
        full, *near = together(gather_hid(summed), *near)
        near_1 = add_far(*far_blocks(inverse(full), "x"), "x")
    with jax.named_scope("scatter"):
        out = [finish_ring(near), finish_direct(near_1)]

    with jax.named_scope("core_swap_out"):
        mine = jnp.where(c == 0, out[0], out[1])
        theirs = fetch(jnp.where(c == 0, out[1], out[0]), "c", 1)
        return jnp.where(
            c == 0,
            jnp.concatenate([mine, theirs], axis=1),
            jnp.concatenate([theirs, mine], axis=1),
        )


def solution(mesh):
    fine = Mesh(mesh.devices.reshape(4, 4, 2, 4, 2), ("x", "zh", "c", "y", "zl"))
    tok = ("x", "zh", "c")
    return jax.shard_map(
        local,
        mesh=fine,
        in_specs=(P(tok, HID), P(tok, HID), P(), P(), P(HID, tok)),
        out_specs=P(tok, HID),
        check_vma=False,
    )
```

```python
import jax
import jax.numpy as jnp
from jax import lax
from jax.experimental import pallas as pl
from jax.experimental.pallas import tpu as pltpu
from jax.sharding import Mesh, PartitionSpec as P

BLOCK = 128
SIZES = {"x": 4, "zh": 4, "c": 2, "y": 4, "zl": 2}
HID = ("y", "zl")
CHUNKS = 2


def fetch(a, axis, d):
    n = SIZES[axis]
    return lax.ppermute(a, axis, [((i + d) % n, i) for i in range(n)])


def near_ring(own, axis):
    return own, fetch(own, axis, 1), fetch(own, axis, -1)


def far_ring(own, ahead, behind, axis):
    half = own.shape[0] // 2
    return own, ahead, fetch(ahead[:half], axis, 1), fetch(behind[half:], axis, -1), behind


def part(a, index, size):
    return lax.dynamic_slice_in_dim(a, index * size, size, 0)


def far_blocks(terms, axis):
    me = lax.axis_index(axis)
    rows = terms.shape[0] // 4
    own, ahead, far, behind = (part(terms, (me + d) % 4, rows) for d in range(4))
    return own, ahead, behind, far[: rows // 2], far[rows // 2 :]


def add_far(own, ahead, behind, far_low, far_high, axis):
    half = own.shape[0] // 2
    to_ahead = fetch(far_low, axis, -1)
    to_behind = fetch(far_high, axis, 1)
    ahead = jnp.concatenate([ahead[:half] + to_ahead, ahead[half:]], axis=0)
    behind = jnp.concatenate([behind[:half], behind[half:] + to_behind], axis=0)
    return own, ahead, behind


def add_near(own, ahead, behind, axis):
    return own + fetch(ahead, axis, -1) + fetch(behind, axis, 1)


def together(*arrays):
    return lax.optimization_barrier(arrays)


def dot(a, b, dims):
    return lax.dot_general(
        a, b, (dims, ((), ())), precision=lax.Precision.HIGH, preferred_element_type=jnp.float32
    )


def halves(a):
    top = a.astype(jnp.bfloat16)
    return top, (a - top.astype(jnp.float32)).astype(jnp.bfloat16)


def split_kernel(core_ref, own_ref, other_ref, full_ref, top_ref, rest_ref):
    width = own_ref.shape[1]
    for ref, columns in ((own_ref, slice(0, width)), (other_ref, slice(width, 2 * width))):
        full_ref[:, columns] = ref[...]
        top_ref[:, columns], rest_ref[:, columns] = halves(ref[...])


def split_matrix(core, rotation, other):
    rows, width = other.shape[0] // 2, other.shape[1]
    tile = 256
    steps = rows // tile
    shape = (rows, 2 * width)
    return pl.pallas_call(
        split_kernel,
        grid_spec=pltpu.PrefetchScalarGridSpec(
            num_scalar_prefetch=1,
            grid=(steps,),
            in_specs=[pl.BlockSpec((tile, width), lambda i, core: (core[0] * steps + i, 0))] * 2,
            out_specs=[pl.BlockSpec((tile, 2 * width), lambda i, core: (i, 0))] * 3,
        ),
        out_shape=[
            jax.ShapeDtypeStruct(shape, jnp.float32),
            jax.ShapeDtypeStruct(shape, jnp.bfloat16),
            jax.ShapeDtypeStruct(shape, jnp.bfloat16),
        ],
        cost_estimate=pl.CostEstimate(
            flops=4 * rows * width, bytes_accessed=24 * rows * width, transcendentals=0
        ),
    )(core.reshape(1), rotation, other)


def mix_kernel(info_ref, base_ref, top_ref, rest_ref, *refs):
    *s_refs, own_ref, other_ref, s_top, s_rest = refs

    def mul(a, b):
        return lax.dot_general(a, b, (((1,), (0,)), ((), ())), preferred_element_type=jnp.float32)

    def rotate(top, rest):
        return mul(top, top_ref[...]) + mul(rest, top_ref[...]) + mul(top, rest_ref[...])

    @pl.when(pl.program_id(0) == 0)
    def _():
        first = 0
        for ref in s_refs:
            rows = slice(first, first + ref.shape[0])
            s_top[rows], s_rest[rows] = halves(ref[...])
            first += ref.shape[0]

    tile, width = own_ref.shape
    spot = info_ref[:, 0:1]
    places = lax.broadcasted_iota(jnp.int32, (tile, s_top.shape[0]), 1)
    pick = jnp.where(places == spot, 1.0, 0.0).astype(jnp.bfloat16)
    source = rotate(mul(pick, s_top[...]).astype(jnp.bfloat16), mul(pick, s_rest[...]).astype(jnp.bfloat16))
    base = rotate(*halves(base_ref[...]))
    lane = lax.broadcasted_iota(jnp.int32, (tile, width), 1)
    own_ref[...] = jnp.where(lane < info_ref[:, 1:2], source[:, :width], base[:, :width])
    other_ref[...] = jnp.where(lane < info_ref[:, 2:3], source[:, width:], base[:, width:])


def mix(chunk, info, base, source, top, rest):
    features = base.shape[1]
    rows = base.shape[0] // CHUNKS
    columns = top.shape[1]
    tile = 256
    steps = rows // tile
    out = jax.ShapeDtypeStruct((rows, columns // 2), jnp.float32)

    def whole(a):
        return pl.BlockSpec(a.shape, lambda i: (0, 0), pipeline_mode=pl.Buffered(1))

    return pl.pallas_call(
        mix_kernel,
        grid=(steps,),
        in_specs=[
            pl.BlockSpec((tile, info.shape[1]), lambda i: (chunk * steps + i, 0)),
            pl.BlockSpec((tile, features), lambda i: (chunk * steps + i, 0)),
            *(whole(a) for a in (top, rest, *source)),
        ],
        out_specs=[pl.BlockSpec((tile, columns // 2), lambda i: (i, 0))] * 2,
        out_shape=[out, out],
        scratch_shapes=[pltpu.VMEM((CHUNKS * rows, features), jnp.bfloat16)] * 2,
        compiler_params=pltpu.CompilerParams(vmem_limit_bytes=48 * 2**20),
        cost_estimate=pl.CostEstimate(
            flops=16 * rows * features * columns, bytes_accessed=24 * rows * features, transcendentals=0
        ),
    )(info, base, top, rest, *source)


def local(base, source, pairs, counts, rotation):
    x, zh, c = (lax.axis_index(a) for a in ("x", "zh", "c"))
    features = rotation.shape[0] // 2
    width = rotation.shape[1]
    rows = base.shape[0]

    with jax.named_scope("core_swap_in"):

        def pick(core):
            picked = [jnp.where(core == 0, a[:, :features], a[:, features:]) for a in (base, source)]
            return jnp.concatenate(picked, axis=0)

        mine = pick(c)
        theirs = fetch(pick(1 - c), "c", 1)
        first = jnp.where(c == 0, mine, theirs)
        second = jnp.where(c == 0, theirs, mine)
        first, second, pairs, counts, rotation = together(first, second, pairs, counts, rotation)

    with jax.named_scope("gather_base"):
        chip_base = jnp.stack([first[:rows], second[:rows]])
        base_all = lax.all_gather(chip_base, ("x", "zh"), axis=1, tiled=True)
        base_all = base_all.reshape(-1, features)

    with jax.named_scope("gather_source"):
        chip_source = jnp.concatenate([first[rows:], second[rows:]], axis=0)
        own, ahead, *far, behind = far_ring(*near_ring(chip_source, "zh"), "zh")
        near = [
            near_ring(jnp.concatenate(blocks, axis=0), "x")
            for blocks in ([own, ahead], [*far, behind])
        ]
        matrix, top, rest = split_matrix(c, rotation, fetch(rotation, "c", 1))
        top, rest, *near[1] = together(top, rest, *near[1])
        source_all = [piece for n in near for piece in far_ring(*n, "x")]

    with jax.named_scope("select"):
        def by_chunk(a):
            return a.reshape(-1, CHUNKS, rows).swapaxes(0, 1).reshape(-1)

        pairs, counts = by_chunk(pairs), by_chunk(counts)
        tok = (x * 4 + zh) * 2
        slot_x = (pairs // 256 - x) % 4
        slot_z = (pairs // 64 - zh) % 4
        spot = slot_z // 2 * 512 + slot_x * 128 + slot_z % 2 * 64 + pairs % 64
        limits = counts * BLOCK
        info = jnp.stack(
            [spot, limits - (tok + c) * width, limits - (tok + 1 - c) * width, spot], axis=1
        )

    def mix_chunk(k, base_all):
        mixed, others = mix(k, info, base_all, source_all, top, rest)
        return mixed + fetch(others, "c", 1)

    chunk = base_all.shape[0] // CHUNKS

    def reduce_hid(m):
        return lax.all_to_all(m.reshape(8, chunk // 8, width), HID, 0, 0).sum(axis=0)

    def gather_hid(m):
        return lax.all_to_all(jnp.broadcast_to(m, (8, *m.shape)), HID, 0, 0).reshape(chunk, width)

    def inverse(full):
        return dot(jnp.concatenate([full, fetch(full, "c", 1)], axis=1), matrix, ((1,), (1,)))

    def finish_ring(near):
        return add_near(*add_far(*far_blocks(add_near(*near, "x"), "zh"), "zh"), "zh")

    def finish_direct(near):
        terms = add_near(*near, "x")
        own, *others = (part(terms, (zh + d) % 4, rows) for d in range(4))
        return own + sum(fetch(a, "zh", -d) for d, a in enumerate(others, 1))

    with jax.named_scope("chunk_0"):
        mixed, base_all = together(mix_chunk(0, base_all), base_all)
        summed = reduce_hid(mixed)
    with jax.named_scope("mix_1"):
        mixed, summed = together(mix_chunk(1, base_all), summed)
    with jax.named_scope("both_chunks"):
        share = chunk // 8
        sent = jnp.concatenate(
            [mixed.reshape(8, share, width), jnp.broadcast_to(summed, (8, share, width))], axis=1
        )
        got = lax.all_to_all(sent, HID, 0, 0)
        summed = got[:, :share].sum(axis=0)
        full = got[:, share:].reshape(chunk, width)
    with jax.named_scope("chunk_0"):
        near = add_far(*together(*far_blocks(inverse(full), "x")), "x")
    with jax.named_scope("chunk_1"):
        full, *near = together(gather_hid(summed), *near)
        near_1 = add_far(*far_blocks(inverse(full), "x"), "x")
    with jax.named_scope("scatter"):
        out = [finish_ring(near), finish_direct(near_1)]

    with jax.named_scope("core_swap_out"):
        mine = jnp.where(c == 0, out[0], out[1])
        theirs = fetch(jnp.where(c == 0, out[1], out[0]), "c", 1)
        return jnp.where(
            c == 0,
            jnp.concatenate([mine, theirs], axis=1),
            jnp.concatenate([theirs, mine], axis=1),
        )


def solution(mesh):
    fine = Mesh(mesh.devices.reshape(4, 4, 2, 4, 2), ("x", "zh", "c", "y", "zl"))
    tok = ("x", "zh", "c")
    return jax.shard_map(
        local,
        mesh=fine,
        in_specs=(P(tok, HID), P(tok, HID), P(), P(), P(HID, tok)),
        out_specs=P(tok, HID),
        check_vma=False,
    )
```

```python
import jax
import jax.numpy as jnp
from jax import lax
from jax.experimental import pallas as pl
from jax.experimental.pallas import tpu as pltpu
from jax.sharding import Mesh, PartitionSpec as P

BLOCK = 128
SIZES = {"x": 4, "zh": 4, "c": 2, "y": 4, "zl": 2}
HID = ("y", "zl")
CHUNKS = 2


def fetch(a, axis, d):
    n = SIZES[axis]
    return lax.ppermute(a, axis, [((i + d) % n, i) for i in range(n)])


def near_ring(own, axis):
    return own, fetch(own, axis, 1), fetch(own, axis, -1)


def far_ring(own, ahead, behind, axis):
    half = own.shape[0] // 2
    return own, ahead, fetch(ahead[:half], axis, 1), fetch(behind[half:], axis, -1), behind


def part(a, index, size):
    return lax.dynamic_slice_in_dim(a, index * size, size, 0)


def far_blocks(terms, axis):
    me = lax.axis_index(axis)
    rows = terms.shape[0] // 4
    own, ahead, far, behind = (part(terms, (me + d) % 4, rows) for d in range(4))
    return own, ahead, behind, far[: rows // 2], far[rows // 2 :]


def add_far(own, ahead, behind, far_low, far_high, axis):
    half = own.shape[0] // 2
    to_ahead = fetch(far_low, axis, -1)
    to_behind = fetch(far_high, axis, 1)
    ahead = jnp.concatenate([ahead[:half] + to_ahead, ahead[half:]], axis=0)
    behind = jnp.concatenate([behind[:half], behind[half:] + to_behind], axis=0)
    return own, ahead, behind


def add_near(own, ahead, behind, axis):
    return own + fetch(ahead, axis, -1) + fetch(behind, axis, 1)


def together(*arrays):
    return lax.optimization_barrier(arrays)


def dot(a, b, dims):
    return lax.dot_general(
        a, b, (dims, ((), ())), precision=lax.Precision.HIGH, preferred_element_type=jnp.float32
    )


def halves(a):
    top = a.astype(jnp.bfloat16)
    return top, (a - top.astype(jnp.float32)).astype(jnp.bfloat16)


def split_kernel(core_ref, own_ref, other_ref, full_ref, top_ref, rest_ref):
    width = own_ref.shape[1]
    for ref, columns in ((own_ref, slice(0, width)), (other_ref, slice(width, 2 * width))):
        full_ref[:, columns] = ref[...]
        top_ref[:, columns], rest_ref[:, columns] = halves(ref[...])


def split_matrix(core, rotation, other):
    rows, width = other.shape[0] // 2, other.shape[1]
    tile = 256
    steps = rows // tile
    shape = (rows, 2 * width)
    return pl.pallas_call(
        split_kernel,
        grid_spec=pltpu.PrefetchScalarGridSpec(
            num_scalar_prefetch=1,
            grid=(steps,),
            in_specs=[pl.BlockSpec((tile, width), lambda i, core: (core[0] * steps + i, 0))] * 2,
            out_specs=[pl.BlockSpec((tile, 2 * width), lambda i, core: (i, 0))] * 3,
        ),
        out_shape=[
            jax.ShapeDtypeStruct(shape, jnp.float32),
            jax.ShapeDtypeStruct(shape, jnp.bfloat16),
            jax.ShapeDtypeStruct(shape, jnp.bfloat16),
        ],
        cost_estimate=pl.CostEstimate(
            flops=4 * rows * width, bytes_accessed=24 * rows * width, transcendentals=0
        ),
    )(core.reshape(1), rotation, other)


def mix_kernel(info_ref, base_ref, top_ref, rest_ref, *refs):
    *s_refs, own_ref, other_ref, s_top, s_rest = refs

    def mul(a, b):
        return lax.dot_general(a, b, (((1,), (0,)), ((), ())), preferred_element_type=jnp.float32)

    def rotate(top, rest):
        return mul(top, top_ref[...]) + mul(rest, top_ref[...]) + mul(top, rest_ref[...])

    @pl.when(pl.program_id(0) == 0)
    def _():
        first = 0
        for ref in s_refs:
            rows = slice(first, first + ref.shape[0])
            s_top[rows], s_rest[rows] = halves(ref[...])
            first += ref.shape[0]

    tile, width = own_ref.shape
    spot = info_ref[:, 0:1]
    places = lax.broadcasted_iota(jnp.int32, (tile, s_top.shape[0]), 1)
    pick = jnp.where(places == spot, 1.0, 0.0).astype(jnp.bfloat16)
    source = rotate(mul(pick, s_top[...]).astype(jnp.bfloat16), mul(pick, s_rest[...]).astype(jnp.bfloat16))
    base = rotate(*halves(base_ref[...]))
    lane = lax.broadcasted_iota(jnp.int32, (tile, width), 1)
    own_ref[...] = jnp.where(lane < info_ref[:, 1:2], source[:, :width], base[:, :width])
    other_ref[...] = jnp.where(lane < info_ref[:, 2:3], source[:, width:], base[:, width:])


def mix(chunk, info, base, source, top, rest):
    features = base.shape[1]
    rows = base.shape[0] // CHUNKS
    columns = top.shape[1]
    tile = 512
    steps = rows // tile
    out = jax.ShapeDtypeStruct((rows, columns // 2), jnp.float32)

    def whole(a):
        return pl.BlockSpec(a.shape, lambda i: (0, 0), pipeline_mode=pl.Buffered(1))

    return pl.pallas_call(
        mix_kernel,
        grid=(steps,),
        in_specs=[
            pl.BlockSpec((tile, info.shape[1]), lambda i: (chunk * steps + i, 0)),
            pl.BlockSpec((tile, features), lambda i: (chunk * steps + i, 0)),
            *(whole(a) for a in (top, rest, *source)),
        ],
        out_specs=[pl.BlockSpec((tile, columns // 2), lambda i: (i, 0))] * 2,
        out_shape=[out, out],
        scratch_shapes=[pltpu.VMEM((CHUNKS * rows, features), jnp.bfloat16)] * 2,
        compiler_params=pltpu.CompilerParams(vmem_limit_bytes=48 * 2**20),
        cost_estimate=pl.CostEstimate(
            flops=16 * rows * features * columns, bytes_accessed=24 * rows * features, transcendentals=0
        ),
    )(info, base, top, rest, *source)


def local(base, source, pairs, counts, rotation):
    x, zh, c = (lax.axis_index(a) for a in ("x", "zh", "c"))
    features = rotation.shape[0] // 2
    width = rotation.shape[1]
    rows = base.shape[0]

    with jax.named_scope("core_swap_in"):

        def pick(core):
            picked = [jnp.where(core == 0, a[:, :features], a[:, features:]) for a in (base, source)]
            return jnp.concatenate(picked, axis=0)

        mine = pick(c)
        theirs = fetch(pick(1 - c), "c", 1)
        first = jnp.where(c == 0, mine, theirs)
        second = jnp.where(c == 0, theirs, mine)
        first, second, pairs, counts, rotation = together(first, second, pairs, counts, rotation)

    with jax.named_scope("gather_base"):
        chip_base = jnp.stack([first[:rows], second[:rows]])
        base_all = lax.all_gather(chip_base, ("x", "zh"), axis=1, tiled=True)
        base_all = base_all.reshape(-1, features)

    with jax.named_scope("gather_source"):
        chip_source = jnp.concatenate([first[rows:], second[rows:]], axis=0)
        own, ahead, *far, behind = far_ring(*near_ring(chip_source, "zh"), "zh")
        near = [
            near_ring(jnp.concatenate(blocks, axis=0), "x")
            for blocks in ([own, ahead], [*far, behind])
        ]
        matrix, top, rest = split_matrix(c, rotation, fetch(rotation, "c", 1))
        top, rest, *near[1] = together(top, rest, *near[1])
        source_all = [piece for n in near for piece in far_ring(*n, "x")]

    with jax.named_scope("select"):
        def by_chunk(a):
            return a.reshape(-1, CHUNKS, rows).swapaxes(0, 1).reshape(-1)

        pairs, counts = by_chunk(pairs), by_chunk(counts)
        tok = (x * 4 + zh) * 2
        slot_x = (pairs // 256 - x) % 4
        slot_z = (pairs // 64 - zh) % 4
        spot = slot_z // 2 * 512 + slot_x * 128 + slot_z % 2 * 64 + pairs % 64
        limits = counts * BLOCK
        info = jnp.stack(
            [spot, limits - (tok + c) * width, limits - (tok + 1 - c) * width, spot], axis=1
        )

    def mix_chunk(k, base_all):
        mixed, others = mix(k, info, base_all, source_all, top, rest)
        return mixed + fetch(others, "c", 1)

    chunk = base_all.shape[0] // CHUNKS

    def reduce_hid(m):
        return lax.all_to_all(m.reshape(8, chunk // 8, width), HID, 0, 0).sum(axis=0)

    def gather_hid(m):
        return lax.all_to_all(jnp.broadcast_to(m, (8, *m.shape)), HID, 0, 0).reshape(chunk, width)

    def inverse(full):
        return dot(jnp.concatenate([full, fetch(full, "c", 1)], axis=1), matrix, ((1,), (1,)))

    def finish_ring(near):
        return add_near(*add_far(*far_blocks(add_near(*near, "x"), "zh"), "zh"), "zh")

    def finish_direct(near):
        terms = add_near(*near, "x")
        own, *others = (part(terms, (zh + d) % 4, rows) for d in range(4))
        return own + sum(fetch(a, "zh", -d) for d, a in enumerate(others, 1))

    with jax.named_scope("chunk_0"):
        mixed, base_all = together(mix_chunk(0, base_all), base_all)
        summed = reduce_hid(mixed)
    with jax.named_scope("mix_1"):
        mixed, summed = together(mix_chunk(1, base_all), summed)
    with jax.named_scope("both_chunks"):
        share = chunk // 8
        sent = jnp.concatenate(
            [mixed.reshape(8, share, width), jnp.broadcast_to(summed, (8, share, width))], axis=1
        )
        got = lax.all_to_all(sent, HID, 0, 0)
        summed = got[:, :share].sum(axis=0)
        full = got[:, share:].reshape(chunk, width)
    with jax.named_scope("chunk_0"):
        near = add_far(*together(*far_blocks(inverse(full), "x")), "x")
    with jax.named_scope("chunk_1"):
        full, *near = together(gather_hid(summed), *near)
        near_1 = add_far(*far_blocks(inverse(full), "x"), "x")
    with jax.named_scope("scatter"):
        out = [finish_ring(near), finish_direct(near_1)]

    with jax.named_scope("core_swap_out"):
        mine = jnp.where(c == 0, out[0], out[1])
        theirs = fetch(jnp.where(c == 0, out[1], out[0]), "c", 1)
        return jnp.where(
            c == 0,
            jnp.concatenate([mine, theirs], axis=1),
            jnp.concatenate([theirs, mine], axis=1),
        )


def solution(mesh):
    fine = Mesh(mesh.devices.reshape(4, 4, 2, 4, 2), ("x", "zh", "c", "y", "zl"))
    tok = ("x", "zh", "c")
    return jax.shard_map(
        local,
        mesh=fine,
        in_specs=(P(tok, HID), P(tok, HID), P(), P(), P(HID, tok)),
        out_specs=P(tok, HID),
        check_vma=False,
    )
```

```python
import jax
import jax.numpy as jnp
from jax import lax
from jax.experimental import pallas as pl
from jax.experimental.pallas import tpu as pltpu
from jax.sharding import Mesh, PartitionSpec as P

BLOCK = 128
SIZES = {"x": 4, "zh": 4, "c": 2, "y": 4, "zl": 2}
HID = ("y", "zl")
CHUNKS = 2


def fetch(a, axis, d):
    n = SIZES[axis]
    return lax.ppermute(a, axis, [((i + d) % n, i) for i in range(n)])


def near_ring(own, axis):
    return own, fetch(own, axis, 1), fetch(own, axis, -1)


def far_ring(own, ahead, behind, axis):
    half = own.shape[0] // 2
    return own, ahead, fetch(ahead[:half], axis, 1), fetch(behind[half:], axis, -1), behind


def part(a, index, size):
    return lax.dynamic_slice_in_dim(a, index * size, size, 0)


def far_blocks(terms, axis):
    me = lax.axis_index(axis)
    rows = terms.shape[0] // 4
    own, ahead, far, behind = (part(terms, (me + d) % 4, rows) for d in range(4))
    return own, ahead, behind, far[: rows // 2], far[rows // 2 :]


def add_far(own, ahead, behind, far_low, far_high, axis):
    half = own.shape[0] // 2
    to_ahead = fetch(far_low, axis, -1)
    to_behind = fetch(far_high, axis, 1)
    ahead = jnp.concatenate([ahead[:half] + to_ahead, ahead[half:]], axis=0)
    behind = jnp.concatenate([behind[:half], behind[half:] + to_behind], axis=0)
    return own, ahead, behind


def add_near(own, ahead, behind, axis):
    return own + fetch(ahead, axis, -1) + fetch(behind, axis, 1)


def together(*arrays):
    return lax.optimization_barrier(arrays)


def dot(a, b, dims):
    return lax.dot_general(
        a, b, (dims, ((), ())), precision=lax.Precision.HIGH, preferred_element_type=jnp.float32
    )


def halves(a):
    top = a.astype(jnp.bfloat16)
    return top, (a - top.astype(jnp.float32)).astype(jnp.bfloat16)


def split_kernel(core_ref, own_ref, other_ref, full_ref, top_ref, rest_ref):
    width = own_ref.shape[1]
    for ref, columns in ((own_ref, slice(0, width)), (other_ref, slice(width, 2 * width))):
        full_ref[:, columns] = ref[...]
        top_ref[:, columns], rest_ref[:, columns] = halves(ref[...])


def split_matrix(core, rotation, other):
    rows, width = other.shape[0] // 2, other.shape[1]
    tile = 256
    steps = rows // tile
    shape = (rows, 2 * width)
    return pl.pallas_call(
        split_kernel,
        grid_spec=pltpu.PrefetchScalarGridSpec(
            num_scalar_prefetch=1,
            grid=(steps,),
            in_specs=[pl.BlockSpec((tile, width), lambda i, core: (core[0] * steps + i, 0))] * 2,
            out_specs=[pl.BlockSpec((tile, 2 * width), lambda i, core: (i, 0))] * 3,
        ),
        out_shape=[
            jax.ShapeDtypeStruct(shape, jnp.float32),
            jax.ShapeDtypeStruct(shape, jnp.bfloat16),
            jax.ShapeDtypeStruct(shape, jnp.bfloat16),
        ],
        cost_estimate=pl.CostEstimate(
            flops=4 * rows * width, bytes_accessed=24 * rows * width, transcendentals=0
        ),
    )(core.reshape(1), rotation, other)


def mix_kernel(info_ref, base_ref, top_ref, rest_ref, *refs):
    *s_refs, own_ref, other_ref, s_top, s_rest = refs

    def mul(a, b):
        return lax.dot_general(a, b, (((1,), (0,)), ((), ())), preferred_element_type=jnp.float32)

    @pl.when(pl.program_id(0) == 0)
    def _():
        first = 0
        for ref in s_refs:
            rows = slice(first, first + ref.shape[0])
            s_top[rows], s_rest[rows] = halves(ref[...])
            first += ref.shape[0]

    tile, width = own_ref.shape
    spot = info_ref[:, 0:1]
    places = lax.broadcasted_iota(jnp.int32, (tile, s_top.shape[0]), 1)
    pick = jnp.where(places == spot, 1.0, 0.0).astype(jnp.bfloat16)
    picked = [mul(pick, s[...]).astype(jnp.bfloat16) for s in (s_top, s_rest)]
    tops, rests = zip(picked, halves(base_ref[...]))
    tops = jnp.concatenate(tops, axis=0)
    sums = mul(jnp.concatenate([tops, *rests], axis=0), top_ref[...])
    sums = sums[: 2 * tile] + sums[2 * tile :] + mul(tops, rest_ref[...])
    source, base = sums[:tile], sums[tile:]
    lane = lax.broadcasted_iota(jnp.int32, (tile, width), 1)
    own_ref[...] = jnp.where(lane < info_ref[:, 1:2], source[:, :width], base[:, :width])
    other_ref[...] = jnp.where(lane < info_ref[:, 2:3], source[:, width:], base[:, width:])


def mix(chunk, info, base, source, top, rest):
    features = base.shape[1]
    rows = base.shape[0] // CHUNKS
    columns = top.shape[1]
    tile = 512
    steps = rows // tile
    out = jax.ShapeDtypeStruct((rows, columns // 2), jnp.float32)

    def whole(a):
        return pl.BlockSpec(a.shape, lambda i: (0, 0), pipeline_mode=pl.Buffered(1))

    return pl.pallas_call(
        mix_kernel,
        grid=(steps,),
        in_specs=[
            pl.BlockSpec((tile, info.shape[1]), lambda i: (chunk * steps + i, 0)),
            pl.BlockSpec((tile, features), lambda i: (chunk * steps + i, 0)),
            *(whole(a) for a in (top, rest, *source)),
        ],
        out_specs=[pl.BlockSpec((tile, columns // 2), lambda i: (i, 0))] * 2,
        out_shape=[out, out],
        scratch_shapes=[pltpu.VMEM((CHUNKS * rows, features), jnp.bfloat16)] * 2,
        compiler_params=pltpu.CompilerParams(vmem_limit_bytes=48 * 2**20),
        cost_estimate=pl.CostEstimate(
            flops=16 * rows * features * columns, bytes_accessed=24 * rows * features, transcendentals=0
        ),
    )(info, base, top, rest, *source)


def local(base, source, pairs, counts, rotation):
    x, zh, c = (lax.axis_index(a) for a in ("x", "zh", "c"))
    features = rotation.shape[0] // 2
    width = rotation.shape[1]
    rows = base.shape[0]

    with jax.named_scope("core_swap_in"):

        def pick(core):
            picked = [jnp.where(core == 0, a[:, :features], a[:, features:]) for a in (base, source)]
            return jnp.concatenate(picked, axis=0)

        mine = pick(c)
        theirs = fetch(pick(1 - c), "c", 1)
        first = jnp.where(c == 0, mine, theirs)
        second = jnp.where(c == 0, theirs, mine)
        first, second, pairs, counts, rotation = together(first, second, pairs, counts, rotation)

    with jax.named_scope("gather_base"):
        chip_base = jnp.stack([first[:rows], second[:rows]])
        base_all = lax.all_gather(chip_base, ("x", "zh"), axis=1, tiled=True)
        base_all = base_all.reshape(-1, features)

    with jax.named_scope("gather_source"):
        chip_source = jnp.concatenate([first[rows:], second[rows:]], axis=0)
        own, ahead, *far, behind = far_ring(*near_ring(chip_source, "zh"), "zh")
        near = [
            near_ring(jnp.concatenate(blocks, axis=0), "x")
            for blocks in ([own, ahead], [*far, behind])
        ]
        matrix, top, rest = split_matrix(c, rotation, fetch(rotation, "c", 1))
        top, rest, *near[1] = together(top, rest, *near[1])
        source_all = [piece for n in near for piece in far_ring(*n, "x")]

    with jax.named_scope("select"):
        def by_chunk(a):
            return a.reshape(-1, CHUNKS, rows).swapaxes(0, 1).reshape(-1)

        pairs, counts = by_chunk(pairs), by_chunk(counts)
        tok = (x * 4 + zh) * 2
        slot_x = (pairs // 256 - x) % 4
        slot_z = (pairs // 64 - zh) % 4
        spot = slot_z // 2 * 512 + slot_x * 128 + slot_z % 2 * 64 + pairs % 64
        limits = counts * BLOCK
        info = jnp.stack(
            [spot, limits - (tok + c) * width, limits - (tok + 1 - c) * width, spot], axis=1
        )

    def mix_chunk(k, base_all):
        mixed, others = mix(k, info, base_all, source_all, top, rest)
        return mixed + fetch(others, "c", 1)

    chunk = base_all.shape[0] // CHUNKS

    def reduce_hid(m):
        return lax.all_to_all(m.reshape(8, chunk // 8, width), HID, 0, 0).sum(axis=0)

    def gather_hid(m):
        return lax.all_to_all(jnp.broadcast_to(m, (8, *m.shape)), HID, 0, 0).reshape(chunk, width)

    def inverse(full):
        return dot(jnp.concatenate([full, fetch(full, "c", 1)], axis=1), matrix, ((1,), (1,)))

    def finish_ring(near):
        return add_near(*add_far(*far_blocks(add_near(*near, "x"), "zh"), "zh"), "zh")

    def finish_direct(near):
        terms = add_near(*near, "x")
        own, *others = (part(terms, (zh + d) % 4, rows) for d in range(4))
        return own + sum(fetch(a, "zh", -d) for d, a in enumerate(others, 1))

    with jax.named_scope("chunk_0"):
        mixed, base_all = together(mix_chunk(0, base_all), base_all)
        summed = reduce_hid(mixed)
    with jax.named_scope("mix_1"):
        mixed, summed = together(mix_chunk(1, base_all), summed)
    with jax.named_scope("both_chunks"):
        share = chunk // 8
        sent = jnp.concatenate(
            [mixed.reshape(8, share, width), jnp.broadcast_to(summed, (8, share, width))], axis=1
        )
        got = lax.all_to_all(sent, HID, 0, 0)
        summed = got[:, :share].sum(axis=0)
        full = got[:, share:].reshape(chunk, width)
    with jax.named_scope("chunk_0"):
        near = add_far(*together(*far_blocks(inverse(full), "x")), "x")
    with jax.named_scope("chunk_1"):
        full, *near = together(gather_hid(summed), *near)
        near_1 = add_far(*far_blocks(inverse(full), "x"), "x")
    with jax.named_scope("scatter"):
        out = [finish_ring(near), finish_direct(near_1)]

    with jax.named_scope("core_swap_out"):
        mine = jnp.where(c == 0, out[0], out[1])
        theirs = fetch(jnp.where(c == 0, out[1], out[0]), "c", 1)
        return jnp.where(
            c == 0,
            jnp.concatenate([mine, theirs], axis=1),
            jnp.concatenate([theirs, mine], axis=1),
        )


def solution(mesh):
    fine = Mesh(mesh.devices.reshape(4, 4, 2, 4, 2), ("x", "zh", "c", "y", "zl"))
    tok = ("x", "zh", "c")
    return jax.shard_map(
        local,
        mesh=fine,
        in_specs=(P(tok, HID), P(tok, HID), P(), P(), P(HID, tok)),
        out_specs=P(tok, HID),
        check_vma=False,
    )
```
